256 devices in a mesh: tm: 16 (over z, core), space: 16 (over x, y).
Axes of the slice: x: 4, y: 4, z: 8, core: 2. Of those that a mesh axis runs over, the one named last changes fastest.
Arguments:
- c_guess: float32 [16, 64, 32, 1024], P('tm', 'space'), may hold values from -6 to 6
- source: float32 [64, 32, 1024], P('space'), may hold values from -4 to 4
- rate: float32 [64, 32, 1024], P('space'), may hold values from 0.25 to 4
Outputs:
- fine_solution: float32 [16, 2, 64, 32, 1024], P('tm', None, 'space')
- coarse_residual: float32 [16, 64, 32, 1024], P('tm', 'space')
The draws below stay inside these ranges and needn't reach their ends.
All inputs are finite; a program needn't handle non-finite values.
Results may differ from the reference program's by a relative error of at most 0.00002.
Values sent between devices are 32-bit elements; how exact they have to be, the bound alone decides.
No kernel may reach another device: no remote copies, remote signals or barrier semaphores. Data moves between devices by JAX's collectives and lax.ppermute only.
A program may use at most 64 MiB of HBM per device.

```python
import math
import jax
import jax.numpy as jnp
from jax import lax

NZ = 32
NY = 1024
M = 2
SWEEPS = 4
NX = 64
N_TM = 16


def shard_levels(own_key, shape, pieces, least, top_value):
    def one(dim, parts):
        steps = jax.random.uniform(jax.random.fold_in(jax.random.fold_in(own_key, 6), dim), (parts,), jnp.float32, least / len(pieces), top_value / len(pieces))
        return jnp.repeat(jnp.exp(steps), shape[dim] // parts).reshape((-1,) + (1,) * (len(shape) - dim - 1))

    factor_of = one(*pieces[0])
    for cut in pieces[1:]:
        factor_of = factor_of * one(*cut)
    return factor_of


def noise(rng, dims, deviation, bound, shards=(), kind=jnp.bfloat16):
    entries = jax.random.normal(rng, dims, jnp.float32) * deviation
    if len(shards) > 0:
        entries = shard_levels(rng, dims, shards, -0.22, 0.18) * entries
    return jnp.clip(entries, min=-bound, max=bound).astype(kind)


def setup_inputs(seed: int = 0) -> dict:
    streams_of = jax.random.split(jax.random.key(seed), 4)
    return {
        "c_guess": noise(streams_of[0], (N_TM, NX, NZ, NY), 1.0, 6.0, ((0, 16), (1, 16)), jnp.float32),
        "source": noise(streams_of[1], (NX, NZ, NY), 0.5, 4.0, ((0, 16),), jnp.float32),
        "rate": jnp.clip(jnp.exp(math.log(4.0) - 2.7725887 * jax.random.uniform(streams_of[2], (NX, NZ, NY), jnp.float32) ** shard_levels(streams_of[2], (NX, NZ, NY), ((0, 16),), -0.2, 0.2)), 0.25, 4.0),
    }


def jacobi_sweep(iterate, right_side, rate_field):
    padded = jnp.pad(iterate, ((0, 0), (1, 1), (1, 1), (1, 1)))
    neighbours = padded[:, 2:, 1:-1, 1:-1] + padded[:, :-2, 1:-1, 1:-1]
    neighbours = neighbours + padded[:, 1:-1, 2:, 1:-1] + padded[:, 1:-1, :-2, 1:-1]
    neighbours = neighbours + padded[:, 1:-1, 1:-1, 2:] + padded[:, 1:-1, 1:-1, :-2]
    return (right_side + rate_field * neighbours) / (1.0 + 6.0 * rate_field)


def implicit_step(state, source_field, rate_field):
    right_side = state if source_field is None else state + source_field
    iterate = state
    for sweep_no in range(SWEEPS):
        iterate = jacobi_sweep(iterate, right_side, rate_field)
    return iterate


def reference(c_guess, source, rate):
    source_all = source[None]
    rate_all = rate[None]
    relaxed = c_guess
    for step_no in range(M - 1):
        relaxed = implicit_step(relaxed, source_all, rate_all)
    stepped = implicit_step(relaxed, source_all, rate_all)
    cpoints = jnp.concatenate([c_guess[:1], stepped[:-1]], 0)
    forward = cpoints
    for step_no in range(M):
        forward = implicit_step(forward, source_all, rate_all)
    zeroed = jnp.zeros_like(cpoints[0])
    residual = jnp.concatenate([zeroed[None], forward[:-1] - cpoints[1:]], 0)
    coarse_rate = M * rate_all

    def chain_turn(error_now, resid_now):
        error_next = implicit_step(error_now[None], None, coarse_rate)[0] + resid_now
        return error_next, error_next

    _, later = lax.scan(chain_turn, zeroed, residual[1:])
    errors = jnp.concatenate([zeroed[None], later], 0)
    fine_points = [cpoints + errors]
    for step_no in range(M - 1):
        fine_points.append(implicit_step(fine_points[-1], source_all, rate_all))
    return jnp.stack(fine_points, 1), residual
```

```python
import functools

import jax
import jax.numpy as jnp
from jax import lax
from jax.experimental import pallas as pl
from jax.experimental.pallas import tpu as pltpu
from jax.sharding import Mesh, PartitionSpec as P

SWEEPS = 4
NT = 16
HALO = 16
CHUNK = 64
WIDE = CHUNK + 2 * HALO
PIECE = 8
STRIP = 4
NZD = 8
NSP = 16
LANES = 128
F32 = jnp.float32

VMEM = pl.BlockSpec(memory_space=pltpu.VMEM)
SMEM = pl.BlockSpec(memory_space=pltpu.SMEM)
LIMIT = 48 * 1024 * 1024


def call(kernel, out, specs, scratch=()):
    outs = [jax.ShapeDtypeStruct(s, F32) for s in out]
    return pl.pallas_call(
        kernel,
        out_shape=outs,
        in_specs=specs,
        out_specs=[VMEM] * len(out),
        scratch_shapes=[pltpu.VMEM(s, F32) for s in scratch],
        compiler_params=pltpu.CompilerParams(vmem_limit_bytes=LIMIT),
    )


SNAKE = [x * 4 + (y if x % 2 == 0 else 3 - y) for x in range(4) for y in range(4)]


def chunk_of_space(j):
    x, y = j // 4, j % 4
    return x * 4 + jnp.where(x % 2 == 0, y, 3 - y)


def flat(z, core, j):
    return (z * 2 + core) * NSP + j


def piece_pairs(first):
    path = [
        (z, SNAKE[k])
        for k in range(NSP)
        for z in (range(NZD) if k % 2 == 0 else range(NZD - 1, -1, -1))
    ]
    pairs = []
    for core in (0, 1):
        for q in range(first, len(path) - 1, 2):
            a = flat(path[q][0], core, path[q][1])
            b = flat(path[q + 1][0], core, path[q + 1][1])
            pairs += [(a, b), (b, a)]
    return pairs


def chunk_pairs(first):
    pairs = []
    for k in range(first, NSP - 1, 2):
        a, b = SNAKE[k], SNAKE[k + 1]
        pairs += [(a, b), (b, a)]
    return pairs


def lateral(v):
    n = v.shape[0]
    x = v.reshape(n * 16, LANES)
    lane = lax.broadcasted_iota(jnp.int32, x.shape, 1)
    row = lax.broadcasted_iota(jnp.int32, x.shape, 0) % 16
    zin = lane % 32
    total = jnp.where(zin < 31, pltpu.roll(x, LANES - 1, 1), 0.0)
    total = total + jnp.where(zin > 0, pltpu.roll(x, 1, 1), 0.0)
    rp = pltpu.roll(x, LANES - 32, 1)
    up = jnp.where(row < 15, pltpu.roll(rp, n * 16 - 1, 0), 0.0)
    total = total + jnp.where(lane >= 96, up, rp)
    rm = pltpu.roll(x, 32, 1)
    dn = jnp.where(row > 0, pltpu.roll(rm, 1, 0), 0.0)
    total = total + jnp.where(lane < 32, dn, rm)
    return total.reshape(v.shape)


def swept(v, bb, cc):
    return bb + cc * (lateral(v[1:-1]) + v[2:] + v[:-2])


def prep_kernel(core_ref, c_ref, s_ref, r_ref, o_ref):
    zero = jnp.zeros((HALO, LANES), F32)

    def spread(load, base):
        for m in range(8):
            tile = load(m).T
            for half in range(2):
                k = 2 * m + half
                part = tile[half * 64 : half * 64 + 64]
                o_ref[SNAKE[k], base + HALO : base + HALO + CHUNK] = part
                if k > 0:
                    o_ref[SNAKE[k - 1], base + HALO + CHUNK : base + WIDE] = part[:HALO]
                if k < NSP - 1:
                    o_ref[SNAKE[k + 1], base : base + HALO] = part[CHUNK - HALO :]
        o_ref[SNAKE[0], base : base + HALO] = zero
        o_ref[SNAKE[NSP - 1], base + HALO + CHUNK : base + WIDE] = zero

    spread(lambda m: c_ref[:, m * 128 : (m + 1) * 128], 0)

    @pl.when(core_ref[0] == 0)
    def _():
        spread(lambda m: s_ref[:, m * 128 : (m + 1) * 128], WIDE)

    @pl.when(core_ref[0] != 0)
    def _():
        spread(lambda m: r_ref[:, m * 128 : (m + 1) * 128], WIDE)


def unpack_kernel(a_ref, c_ref, q_ref):
    def one(y, _):
        c_ref[y] = a_ref[pl.ds(y, NSP, stride=2 * WIDE), :]
        q_ref[y] = a_ref[pl.ds(WIDE + y, NSP, stride=2 * WIDE), :]
        return 0

    lax.fori_loop(0, WIDE, one, 0, unroll=8)


def fine_kernel(
    info_ref, c_ref, own_ref, oth_ref, o_ref, inv2_ref, cc2_ref, inv_ref, cc_ref, sinv_ref,
    a_ref, b_ref, bb_ref, rate_ref,
):
    core = info_ref[0]
    odd = info_ref[1]
    sub = info_ref[2]
    step = 8

    def init(n, _):
        at = pl.ds(pl.multiple_of(n * step, step), step)
        own, oth = own_ref[at], oth_ref[at]
        source = jnp.where(core == 0, own, oth)
        rate = jnp.where(core == 0, oth, own)
        inv = 1.0 / (1.0 + 6.0 * rate)
        rate_ref[at] = rate
        inv_ref[at] = inv
        cc_ref[at] = rate * inv
        sinv_ref[at] = source * inv
        a_ref[pl.ds(n * step + 1, step)] = c_ref[at]
        return 0

    lax.fori_loop(0, WIDE // step, init, 0)

    refs = [a_ref, b_ref]
    for number in range(4):
        def right(n, _):
            at = pl.ds(pl.multiple_of(n * step, step), step)
            bb_ref[at] = a_ref[pl.ds(n * step + 1, step)] * inv_ref[at] + sinv_ref[at]
            return 0

        lax.fori_loop(0, WIDE // step, right, 0)
        for sweep in range(SWEEPS):
            src, dst = refs[sweep % 2], refs[(sweep + 1) % 2]
            low = number * SWEEPS + sweep + 1
            blocks = -(-(WIDE - 2 * low) // step)
            start = WIDE // 2 - blocks * step // 2

            def block(n, _, src=src, dst=dst, start=start):
                at = start + n * step
                v = src[pl.ds(at, step + 2)]
                dst[pl.ds(at + 1, step)] = swept(v, bb_ref[pl.ds(at, step)], cc_ref[pl.ds(at, step)])
                return 0

            lax.fori_loop(0, blocks, block, 0)
        if number % 2 == 1:
            for z in range(NZD):
                part = jnp.where(odd == 1, NZD - 1 - z, z)
                o_ref[z, number // 2] = a_ref[pl.ds(HALO + 1 + PIECE * part, PIECE)]

    rate = 2.0 * rate_ref[pl.ds(HALO - PIECE + PIECE * sub, 3 * PIECE)]
    inv = 1.0 / (1.0 + 6.0 * rate)
    inv2_ref[...] = inv
    cc2_ref[...] = rate * inv


def messages(odd, e, r_next, a_ref, b_ref):
    head, tail = r_next[:STRIP], r_next[STRIP:]
    a_ref[:PIECE] = e
    b_ref[:PIECE] = e
    a_ref[PIECE:] = jnp.where(odd == 0, tail, head)
    b_ref[PIECE:] = jnp.where(odd == 0, head, tail)


def residual_kernel(info_ref, own_ref, oth_ref, r_ref, cp_ref, mine_ref, a_ref, b_ref):
    core, odd = info_ref[0], info_ref[3]

    def uw(t, which):
        mine, other = own_ref[t // 2, which], oth_ref[t // 2, which]
        return jnp.where(core == t % 2, mine, other)

    r_ref[0] = jnp.zeros(r_ref.shape[1:], F32)
    r_ref[1] = uw(0, 0) - uw(0, 0)
    for t in range(2, NT):
        r_ref[t] = uw(t - 2, 1) - uw(t - 1, 0)
    for n in range(NT // 2):
        even_cp = oth_ref[max(n - 1, 0), 0]
        cp_ref[n] = jnp.where(core == 0, even_cp, oth_ref[n, 0])
        mine_ref[n] = jnp.where(core == 0, r_ref[2 * n], r_ref[2 * n + 1])
    messages(odd, r_ref[1], r_ref[2], a_ref, b_ref)


def coarse_step(v, inv, cc):
    bb = v * inv
    for sweep in range(SWEEPS):
        low = sweep + 1
        high = bb.shape[0] - low
        v = swept(v, bb[low:high], cc[low:high])
    return v


def chain_kernel(t, info_ref, ra_ref, rb_ref, e_ref, r_ref, inv_ref, cc_ref, e1_ref, e2_ref, *out):
    odd = info_ref[3]
    ra, rb = ra_ref[...], rb_ref[...]
    left = jnp.where(odd == 0, rb, ra)
    right = jnp.where(odd == 0, ra, rb)
    e = jnp.concatenate([left[:PIECE], e_ref[...], right[:PIECE]], 0)
    r1 = jnp.concatenate([left[PIECE:], r_ref[t + 1], right[PIECE:]], 0)
    inv, cc = inv_ref[...], cc_ref[...]
    e1 = coarse_step(e, inv, cc) + r1
    e2 = coarse_step(e1, inv[STRIP:-STRIP], cc[STRIP:-STRIP]) + r_ref[t + 2]
    e1_ref[...] = e1[STRIP:-STRIP]
    e2_ref[...] = e2
    if out:
        messages(odd, e2, r_ref[t + 3], *out)


def correct_kernel(info_ref, cp_ref, r_ref, *refs):
    core = info_ref[0]
    e_refs, o_ref = refs[:-1], refs[-1]
    for n in range(NT // 2):
        even = e_refs[2 * n - 1][...] if n > 0 else jnp.zeros(cp_ref.shape[1:], F32)
        o_ref[n, 0] = cp_ref[n] + jnp.where(core == 0, even, e_refs[2 * n][...])
        o_ref[n, 1] = r_ref[n]


def last_kernel(info_ref, g_ref, c_ref, ra_ref, rb_ref, inv_ref, cc_ref, sinv_ref, o_ref, a_ref, b_ref, bb_ref):
    odd, first = info_ref[1], info_ref[4]
    size = CHUNK + 2 * STRIP
    step = 8
    for n in range(NZD):
        z = jnp.where(odd == 1, NZD - 1 - n, n)
        c = c_ref[HALO + n * PIECE : HALO + n * PIECE + PIECE]
        a_ref[1 + STRIP + n * PIECE : 1 + STRIP + (n + 1) * PIECE] = jnp.where(first == 1, c, g_ref[z, 0])
        for y in range(PIECE):
            o_ref[pl.ds(2 * CHUNK + n * PIECE + y, NSP, stride=3 * CHUNK), :] = g_ref[z, 1, y]
    a_ref[1 : 1 + STRIP] = jnp.where(odd == 0, rb_ref[...], ra_ref[...])
    a_ref[1 + STRIP + CHUNK : 1 + size] = jnp.where(odd == 0, ra_ref[...], rb_ref[...])

    off = HALO - STRIP

    def right(n, _):
        at = n * step
        v = a_ref[pl.ds(at + 1, step)]
        bb_ref[pl.ds(at, step)] = v * inv_ref[pl.ds(off + at, step)] + sinv_ref[pl.ds(off + at, step)]
        return 0

    lax.fori_loop(0, size // step, right, 0)

    def keep(which):
        def one(y, _):
            o_ref[pl.ds(which * CHUNK + y, NSP, stride=3 * CHUNK), :] = a_ref[1 + STRIP + y]
            return 0

        lax.fori_loop(0, CHUNK, one, 0, unroll=8)

    keep(0)
    refs = [a_ref, b_ref]
    for sweep in range(SWEEPS):
        src, dst = refs[sweep % 2], refs[(sweep + 1) % 2]
        blocks = -(-(size - 2 * (sweep + 1)) // step)
        start = size // 2 - blocks * step // 2

        def block(n, _, src=src, dst=dst, start=start):
            at = start + n * step
            v = src[pl.ds(at, step + 2)]
            dst[pl.ds(at + 1, step)] = swept(
                v, bb_ref[pl.ds(at, step)], cc_ref[pl.ds(off + at, step)]
            )
            return 0

        lax.fori_loop(0, blocks, block, 0)
    keep(1)


def finish_kernel(a_ref, f_ref, r_ref):
    outs = [f_ref.at[0], f_ref.at[1], r_ref]
    for which in range(3):
        for m in range(8):
            low = a_ref[SNAKE[2 * m], which * CHUNK : (which + 1) * CHUNK]
            high = a_ref[SNAKE[2 * m + 1], which * CHUNK : (which + 1) * CHUNK]
            outs[which][:, m * 128 : (m + 1) * 128] = jnp.concatenate([low, high], 0).T


def body(c_guess, source, rate):
    z = lax.axis_index("z")
    core = lax.axis_index("core")
    k = chunk_of_space(lax.axis_index("space"))
    odd_chunk = k % 2
    sub = jnp.where(odd_chunk == 1, NZD - 1 - z, z)
    first = jnp.where((z == 0) & (core == 0), 1, 0)
    info = jnp.stack([core, odd_chunk, sub, sub % 2, first]).astype(jnp.int32)
    everyone = ("z", "core", "space")

    def swap(v):
        return lax.ppermute(v, "core", [(0, 1), (1, 0)])

    plane = (16, LANES)

    sent = call(prep_kernel, [(NSP, 2 * WIDE, LANES)], [SMEM] + [VMEM] * 3)(
        info, c_guess.reshape(LANES, -1), source.reshape(LANES, -1), rate.reshape(LANES, -1)
    )[0]
    got = lax.all_to_all(sent, "space", 0, 0)
    c, own = call(unpack_kernel, [(WIDE,) + plane] * 2, [VMEM])(got.reshape(-1, LANES))
    oth = swap(own)

    uw, inv2, cc2, inv, cc, sinv = call(
        fine_kernel,
        [(NZD, 2, PIECE) + plane] + [(3 * PIECE,) + plane] * 2 + [(WIDE,) + plane] * 3,
        [SMEM] + [VMEM] * 3,
        [(WIDE + 2,) + plane] * 2 + [(WIDE,) + plane] * 2,
    )(info, c, own, oth)

    mine = lax.all_to_all(uw, "z", 0, 0)
    other = swap(mine)
    piece = (PIECE,) + plane
    message = (PIECE + STRIP,) + plane
    res, cpoint, res_mine, ma, mb = call(
        residual_kernel,
        [(NT,) + piece, (NT // 2,) + piece, (NT // 2,) + piece, message, message],
        [SMEM] + [VMEM] * 2,
    )(info, mine, other)

    errors = [res[1]]
    pairs_a, pairs_b = piece_pairs(0), piece_pairs(1)
    for t in range(1, NT - 1, 2):
        ra = lax.ppermute(ma, everyone, pairs_a)
        rb = lax.ppermute(mb, everyone, pairs_b)
        last = t + 2 == NT - 1
        made = call(
            functools.partial(chain_kernel, t),
            [piece, piece] + ([] if last else [message, message]),
            [SMEM] + [VMEM] * 6,
        )(info, ra, rb, errors[-1], res, inv2, cc2)
        errors += made[:2]
        if not last:
            ma, mb = made[2:]

    corrected = call(
        correct_kernel, [(NZD, 2) + piece], [SMEM] + [VMEM] * (2 + len(errors))
    )(info, cpoint, res_mine, *errors)[0]
    chunk = lax.all_to_all(corrected, "z", 0, 0)
    head = jnp.where(odd_chunk == 0, chunk[0, 0, :STRIP], chunk[NZD - 1, 0, :STRIP])
    tail = jnp.where(odd_chunk == 0, chunk[NZD - 1, 0, STRIP:], chunk[0, 0, STRIP:])
    head = jnp.where(first == 1, c[HALO : HALO + STRIP], head)
    tail = jnp.where(first == 1, c[HALO + CHUNK - STRIP : HALO + CHUNK], tail)
    ra = lax.ppermute(jnp.where(odd_chunk == 0, tail, head), "space", chunk_pairs(0))
    rb = lax.ppermute(jnp.where(odd_chunk == 0, head, tail), "space", chunk_pairs(1))
    size = CHUNK + 2 * STRIP
    sent = call(
        last_kernel,
        [(NSP * 3 * CHUNK, LANES)],
        [SMEM] + [VMEM] * 7,
        [(size + 2,) + plane] * 2 + [(size,) + plane],
    )(info, chunk, c, ra, rb, inv, cc, sinv)[0]
    got = lax.all_to_all(sent.reshape(NSP, 3 * CHUNK, LANES), "space", 0, 0)
    fine, residual = call(finish_kernel, [(2, LANES, 1024), (LANES, 1024)], [VMEM])(got)
    return fine.reshape(1, 2, 4, 32, 1024), residual.reshape(1, 4, 32, 1024)


def solution(mesh):
    inner = Mesh(mesh.devices.reshape(NZD, 2, NSP), ("z", "core", "space"))
    tm = ("z", "core")
    return jax.shard_map(
        body,
        mesh=inner,
        in_specs=(P(tm, "space", None, None), P("space", None, None), P("space", None, None)),
        out_specs=(P(tm, None, "space", None, None), P(tm, "space", None, None)),
        check_vma=False,
    )
```

```python
import functools

import jax
import jax.numpy as jnp
from jax import lax
from jax.experimental import pallas as pl
from jax.experimental.pallas import tpu as pltpu
from jax.sharding import Mesh, PartitionSpec as P

SWEEPS = 4
NT = 16
HALO = 16
CHUNK = 64
WIDE = CHUNK + 2 * HALO
PIECE = 8
STRIP = 4
NZD = 8
NSP = 16
LANES = 128
F32 = jnp.float32

VMEM = pl.BlockSpec(memory_space=pltpu.VMEM)
LIMIT = 16 * 1024 * 1024
MOST = 60 * 1024 * 1024
BF16 = jnp.bfloat16


def call(kernel, out, specs, scratch=(), mixer=False, sems=0, limit=LIMIT):
    outs = [jax.ShapeDtypeStruct(s, F32) for s in out]
    scratch = [pltpu.VMEM(s, F32) for s in scratch]
    if mixer:
        scratch.append(pltpu.VMEM((2 * LANES, 2 * LANES), BF16))
    if sems:
        scratch.append(pltpu.SemaphoreType.DMA((sems,)))
    return pl.pallas_call(
        kernel,
        out_shape=outs,
        in_specs=specs,
        out_specs=[VMEM] * len(out),
        scratch_shapes=scratch,
        compiler_params=pltpu.CompilerParams(vmem_limit_bytes=limit),
    )


SNAKE = [x * 4 + (y if x % 2 == 0 else 3 - y) for x in range(4) for y in range(4)]


def position():
    z, core = lax.axis_index("z"), lax.axis_index("core")
    j = lax.axis_index("space")
    x = j // 4
    odd = x % 2
    y = j % 4
    odd_chunk = (y + odd) % 2
    sub = z + odd_chunk * (NZD - 1 - 2 * z)
    return z, core, odd_chunk, sub


def flat(z, core, j):
    return (z * 2 + core) * NSP + j


def piece_pairs(first):
    path = [
        (z, SNAKE[k])
        for k in range(NSP)
        for z in (range(NZD) if k % 2 == 0 else range(NZD - 1, -1, -1))
    ]
    pairs = []
    for core in (0, 1):
        for q in range(first, len(path) - 1, 2):
            a = flat(path[q][0], core, path[q][1])
            b = flat(path[q + 1][0], core, path[q + 1][1])
            pairs += [(a, b), (b, a)]
    return pairs


def chunk_pairs(first):
    pairs = []
    for z in range(NZD):
        for core in (0, 1):
            for k in range(first, NSP - 1, 2):
                a, b = flat(z, core, SNAKE[k]), flat(z, core, SNAKE[k + 1])
                pairs += [(a, b), (b, a)]
    return pairs


def edges(rows):
    shape = (1, rows, LANES)
    lane = lax.broadcasted_iota(jnp.int32, shape, 2)
    row = lax.broadcasted_iota(jnp.int32, shape, 1)
    top, bottom = (lane >= 96) & (row < 15), (lane < 32) & (row > 0)
    return (lane & 31) < 31, (lane & 31) > 0, lane >= 96, lane < 32, top, bottom


def rolled(v):
    z_top, z_bottom, x_top, x_bottom, top, bottom = edges(16)
    total = jnp.where(z_top, pltpu.roll(v, LANES - 1, 2), 0.0)
    total = total + jnp.where(z_bottom, pltpu.roll(v, 1, 2), 0.0)
    up = pltpu.roll(v, LANES - 32, 2)
    down = pltpu.roll(v, 32, 2)
    far_up = jnp.where(top, pltpu.roll(up, 15, 1), 0.0)
    far_down = jnp.where(bottom, pltpu.roll(down, 1, 1), 0.0)
    return total + jnp.where(x_top, far_up, up) + jnp.where(x_bottom, far_down, down)


def fill_mixer(m_ref):
    shape = (2 * LANES, 2 * LANES)
    source = lax.broadcasted_iota(jnp.int32, shape, 0) & (LANES - 1)
    column = lax.broadcasted_iota(jnp.int32, shape, 1)
    lane = column & (LANES - 1)
    apart = jnp.abs(source - lane)
    near = ((apart == 1) & ((source >> 5) == (lane >> 5))) | (apart == 32)
    far = apart == 96
    picked = jnp.where(column < LANES, jnp.where(near, 1.0, 0.0), jnp.where(far, 1.0, 0.0))
    m_ref[...] = picked.astype(BF16)


def mixed(v, m_ref):
    n = v.shape[0]
    _, _, _, _, top, bottom = edges(16)
    x = v.reshape(n * 16, LANES)
    high = x.astype(BF16)
    rest = x - high.astype(F32)
    middle = rest.astype(BF16)
    low = (rest - middle.astype(F32)).astype(BF16)
    both = jnp.concatenate([high, middle], 1)
    p = jnp.dot(both, m_ref[...], preferred_element_type=F32)
    p = p + jnp.dot(low, m_ref[:LANES], preferred_element_type=F32)
    near = p[:, :LANES].reshape(v.shape)
    far = p[:, LANES:].reshape(v.shape)
    across = jnp.where(bottom, pltpu.roll(far, 1, 1), 0.0)
    return near + jnp.where(top, pltpu.roll(far, 15, 1), across)


def lateral(v, m_ref):
    if m_ref is None:
        return rolled(v)
    cut = v.shape[0] // 3
    return jnp.concatenate([rolled(v[:cut]), mixed(v[cut:], m_ref)], 0)


def swept(v, bb, cc, m_ref=None):
    return bb + cc * (lateral(v[1:-1], m_ref) + v[2:] + v[:-2])


def prep_kernel(c_ref, s_ref, r_ref, o_ref, v_ref, q_ref, sems):
    core = lax.axis_index("core")
    zero = jnp.zeros((HALO, LANES), F32)

    def copies(ref, to, first):
        return [
            pltpu.make_async_copy(
                ref.at[:, pl.ds(m * LANES, LANES)], to.at[:, pl.ds(m * LANES, LANES)], sems.at[first + m]
            )
            for m in range(8)
        ]

    def spread(arriving, ref, base):
        for m in range(8):
            arriving[m].wait()
            tile = ref[:, m * LANES : (m + 1) * LANES].T
            for half in range(2):
                k = 2 * m + half
                part = tile[half * 64 : half * 64 + 64]
                o_ref[SNAKE[k], base + HALO : base + HALO + CHUNK] = part
                if k > 0:
                    o_ref[SNAKE[k - 1], base + HALO + CHUNK : base + WIDE] = part[:HALO]
                if k < NSP - 1:
                    o_ref[SNAKE[k + 1], base : base + HALO] = part[CHUNK - HALO :]
        o_ref[SNAKE[0], base : base + HALO] = zero
        o_ref[SNAKE[NSP - 1], base + HALO + CHUNK : base + WIDE] = zero

    states = copies(c_ref, v_ref, 0)
    for copy in states:
        copy.start()

    @pl.when(core == 0)
    def _():
        fields = copies(s_ref, q_ref, 8)
        for copy in fields:
            copy.start()
        spread(fields, q_ref, WIDE)

    @pl.when(core != 0)
    def _():
        fields = copies(r_ref, q_ref, 8)
        for copy in fields:
            copy.start()
        spread(fields, q_ref, WIDE)

    spread(states, v_ref, 0)


def unpack_kernel(a_ref, q_ref):
    def one(y, _):
        q_ref[y] = a_ref[pl.ds(WIDE + y, NSP, stride=2 * WIDE), :]
        return 0

    lax.fori_loop(0, WIDE, one, 0, unroll=8)


def fine_kernel(
    g_ref, own_ref, oth_ref, o_ref, inv2_ref, cc2_ref, inv_ref, cc_ref, sinv_ref, c_ref,
    a_ref, b_ref, bb_ref, rate_ref, m_ref,
):
    _, core, odd, sub = position()
    step = 8
    fill_mixer(m_ref)

    def gather(y, _):
        a_ref[y] = g_ref[pl.ds(y, NSP, stride=2 * WIDE), :]
        return 0

    lax.fori_loop(0, WIDE, gather, 0, unroll=8)
    c_ref[...] = a_ref[HALO : HALO + CHUNK]

    def init(n, _):
        at = pl.ds(pl.multiple_of(n * step, step), step)
        own, oth = own_ref[at], oth_ref[at]
        source = jnp.where(core == 0, own, oth)
        rate = jnp.where(core == 0, oth, own)
        inv = 1.0 / (1.0 + 6.0 * rate)
        rate_ref[at] = rate
        inv_ref[at] = inv
        cc_ref[at] = rate * inv
        sinv_ref[at] = source * inv
        return 0

    lax.fori_loop(0, WIDE // step, init, 0)

    refs = [a_ref, b_ref]
    for number in range(4):
        def right(n, _):
            at = pl.ds(pl.multiple_of(n * step, step), step)
            bb_ref[at] = a_ref[at] * inv_ref[at] + sinv_ref[at]
            return 0

        lax.fori_loop(0, WIDE // step, right, 0)
        for sweep in range(SWEEPS):
            src, dst = refs[sweep % 2], refs[(sweep + 1) % 2]
            low = number * SWEEPS + sweep + 1
            high = WIDE - low
            dst[low:high] = swept(src[low - 1 : high + 1], bb_ref[low:high], cc_ref[low:high], m_ref)
        if number % 2 == 1:
            for z in range(NZD):
                part = jnp.where(odd == 1, NZD - 1 - z, z)
                o_ref[z, number // 2] = a_ref[pl.ds(HALO + PIECE * part, PIECE)]

    rate = 2.0 * rate_ref[pl.ds(HALO - PIECE + PIECE * sub, 3 * PIECE)]
    inv = 1.0 / (1.0 + 6.0 * rate)
    inv2_ref[...] = inv
    cc2_ref[...] = rate * inv


def messages(odd, e, r_next, a_ref, b_ref):
    head, tail = r_next[:STRIP], r_next[STRIP:]
    a_ref[:PIECE] = e
    b_ref[:PIECE] = e
    a_ref[PIECE:] = jnp.where(odd == 0, tail, head)
    b_ref[PIECE:] = jnp.where(odd == 0, head, tail)


def residual_kernel(own_ref, oth_ref, r_ref, cp_ref, mine_ref, a_ref, b_ref):
    _, core, _, sub = position()
    odd = sub % 2

    def uw(t, which):
        mine, other = own_ref[t // 2, which], oth_ref[t // 2, which]
        return jnp.where(core == t % 2, mine, other)

    r_ref[0] = jnp.zeros(r_ref.shape[1:], F32)
    r_ref[1] = uw(0, 0) - uw(0, 0)
    for t in range(2, NT):
        r_ref[t] = uw(t - 2, 1) - uw(t - 1, 0)
    for n in range(NT // 2):
        even_cp = oth_ref[max(n - 1, 0), 0]
        cp_ref[n] = jnp.where(core == 0, even_cp, oth_ref[n, 0])
        mine_ref[n] = jnp.where(core == 0, r_ref[2 * n], r_ref[2 * n + 1])
    messages(odd, r_ref[1], r_ref[2], a_ref, b_ref)


def coarse_step(v, inv, cc):
    bb = v * inv
    for sweep in range(SWEEPS):
        low = sweep + 1
        high = bb.shape[0] - low
        v = swept(v, bb[low:high], cc[low:high])
    return v


def chain_step(t, ra_ref, rb_ref, e_ref, r_ref, inv_ref, cc_ref):
    sub = position()[3]
    odd = sub % 2
    ra, rb = ra_ref[...], rb_ref[...]
    left = jnp.where(odd == 0, rb, ra)
    right = jnp.where(odd == 0, ra, rb)
    e = jnp.concatenate([left[:PIECE], e_ref[...], right[:PIECE]], 0)
    r1 = jnp.concatenate([left[PIECE:], r_ref[t + 1], right[PIECE:]], 0)
    inv, cc = inv_ref[...], cc_ref[...]
    e1 = coarse_step(e, inv, cc) + r1
    e2 = coarse_step(e1, inv[STRIP:-STRIP], cc[STRIP:-STRIP]) + r_ref[t + 2]
    return e1[STRIP:-STRIP], e2


def chain_kernel(t, ra_ref, rb_ref, e_ref, r_ref, inv_ref, cc_ref, e1_ref, e2_ref, a_ref, b_ref):
    sub = position()[3]
    e1, e2 = chain_step(t, ra_ref, rb_ref, e_ref, r_ref, inv_ref, cc_ref)
    e1_ref[...] = e1
    e2_ref[...] = e2
    messages(sub % 2, e2, r_ref[t + 3], a_ref, b_ref)


def chain_end_kernel(t, ra_ref, rb_ref, r_ref, inv_ref, cc_ref, cp_ref, mine_ref, *refs):
    core = lax.axis_index("core")
    e_refs, o_ref = refs[:-1], refs[-1]
    e1, e2 = chain_step(t, ra_ref, rb_ref, e_refs[-1], r_ref, inv_ref, cc_ref)
    errors = [jnp.zeros(e1.shape, F32)] + [ref[...] for ref in e_refs] + [e1, e2]
    for n in range(NT // 2):
        o_ref[n, 0] = cp_ref[n] + jnp.where(core == 0, errors[2 * n], errors[2 * n + 1])
        o_ref[n, 1] = mine_ref[n]


def last_kernel(
    g_ref, c_ref, ra_ref, rb_ref, inv_ref, cc_ref, sinv_ref, o_ref, a_ref, b_ref, bb_ref, m_ref, sems
):
    device_z, core, odd, _ = position()
    size = CHUNK + 2 * STRIP
    fill_mixer(m_ref)
    for n in range(NZD):
        z = jnp.where(odd == 1, NZD - 1 - n, n)
        a_ref[STRIP + n * PIECE : STRIP + (n + 1) * PIECE] = g_ref[z, 0]
        for y in range(PIECE):
            o_ref[pl.ds(2 * CHUNK + n * PIECE + y, NSP, stride=3 * CHUNK), :] = g_ref[z, 1, y]
    a_ref[:STRIP] = jnp.where(odd == 0, rb_ref[...], ra_ref[...])
    a_ref[STRIP + CHUNK : size] = jnp.where(odd == 0, ra_ref[...], rb_ref[...])

    @pl.when((device_z == 0) & (core == 0))
    def _():
        copy = pltpu.make_async_copy(c_ref, a_ref.at[pl.ds(STRIP, CHUNK)], sems.at[0])
        copy.start()
        copy.wait()

    off = HALO - STRIP
    bb_ref[...] = a_ref[...] * inv_ref[off : off + size] + sinv_ref[off : off + size]

    def keep(which):
        def one(y, _):
            o_ref[pl.ds(which * CHUNK + y, NSP, stride=3 * CHUNK), :] = a_ref[STRIP + y]
            return 0

        lax.fori_loop(0, CHUNK, one, 0, unroll=8)

    keep(0)
    refs = [a_ref, b_ref]
    for sweep in range(SWEEPS):
        src, dst = refs[sweep % 2], refs[(sweep + 1) % 2]
        low = sweep + 1
        high = size - low
        dst[low:high] = swept(
            src[low - 1 : high + 1], bb_ref[low:high], cc_ref[off + low : off + high], m_ref
        )
    keep(1)


def finish_kernel(a_ref, f_ref, r_ref):
    outs = [f_ref.at[0], f_ref.at[1], r_ref]
    for which in range(3):
        for m in range(8):
            low = a_ref[SNAKE[2 * m], which * CHUNK : (which + 1) * CHUNK]
            high = a_ref[SNAKE[2 * m + 1], which * CHUNK : (which + 1) * CHUNK]
            outs[which][:, m * 128 : (m + 1) * 128] = jnp.concatenate([low, high], 0).T


def strips_kernel(g_ref, c_ref, a_ref, b_ref, head_ref, tail_ref, sems):
    z, core, odd, _ = position()
    low, high = odd * (NZD - 1), (1 - odd) * (NZD - 1)
    head_ref[...] = g_ref[low, 0, :STRIP]
    tail_ref[...] = g_ref[high, 0, STRIP:]

    @pl.when((z == 0) & (core == 0))
    def _():
        copies = [
            pltpu.make_async_copy(c_ref.at[pl.ds(0, STRIP)], head_ref, sems.at[0]),
            pltpu.make_async_copy(c_ref.at[pl.ds(CHUNK - STRIP, STRIP)], tail_ref, sems.at[1]),
        ]
        for copy in copies:
            copy.start()
        for copy in copies:
            copy.wait()

    head, tail = head_ref[...], tail_ref[...]
    a_ref[...] = jnp.where(odd == 0, tail, head)
    b_ref[...] = jnp.where(odd == 0, head, tail)


def body(c_guess, source, rate):
    everyone = ("z", "core", "space")
    anywhere = pl.BlockSpec(memory_space=pltpu.HBM)
    plane = (16, LANES)
    piece = (PIECE,) + plane
    message = (PIECE + STRIP,) + plane

    def swap(v):
        return lax.ppermute(v, "core", [(0, 1), (1, 0)])

    sent = call(
        prep_kernel, [(NSP, 2 * WIDE, LANES)], [anywhere] * 3, [(LANES, 1024)] * 2, sems=16, limit=MOST
    )(c_guess.reshape(LANES, -1), source.reshape(LANES, -1), rate.reshape(LANES, -1))[0]
    got = lax.all_to_all(sent, "space", 0, 0).reshape(-1, LANES)
    own = call(unpack_kernel, [(WIDE,) + plane], [VMEM])(got)[0]
    oth = swap(own)

    uw, inv2, cc2, inv, cc, sinv, c = call(
        fine_kernel,
        [(NZD, 2) + piece]
        + [(3 * PIECE,) + plane] * 2
        + [(WIDE,) + plane] * 3
        + [(CHUNK,) + plane],
        [VMEM] * 3,
        [(WIDE,) + plane] * 4,
        mixer=True,
    )(got, own, oth)

    mine = lax.all_to_all(uw, "z", 0, 0)
    other = swap(mine)
    res, cpoint, res_mine, ma, mb = call(
        residual_kernel,
        [(NT,) + piece, (NT // 2,) + piece, (NT // 2,) + piece, message, message],
        [VMEM] * 2,
    )(mine, other)

    pairs_a, pairs_b = piece_pairs(0), piece_pairs(1)
    errors = [res[1]]
    for t in range(1, NT - 3, 2):
        ra = lax.ppermute(ma, everyone, pairs_a)
        rb = lax.ppermute(mb, everyone, pairs_b)
        e1, e2, ma, mb = call(
            functools.partial(chain_kernel, t), [piece, piece, message, message], [VMEM] * 6
        )(ra, rb, errors[-1], res, inv2, cc2)
        errors += [e1, e2]
    ra = lax.ppermute(ma, everyone, pairs_a)
    rb = lax.ppermute(mb, everyone, pairs_b)
    corrected = call(
        functools.partial(chain_end_kernel, NT - 3),
        [(NZD, 2) + piece],
        [VMEM] * (7 + len(errors)),
    )(ra, rb, res, inv2, cc2, cpoint, res_mine, *errors)[0]

    chunk = lax.all_to_all(corrected, "z", 0, 0)
    edge = (STRIP,) + plane
    ma, mb = call(strips_kernel, [edge] * 2, [VMEM, anywhere], [edge] * 2, sems=2)(chunk, c)
    ra = lax.ppermute(ma, everyone, chunk_pairs(0))
    rb = lax.ppermute(mb, everyone, chunk_pairs(1))
    size = CHUNK + 2 * STRIP
    sent = call(
        last_kernel,
        [(NSP * 3 * CHUNK, LANES)],
        [VMEM, anywhere] + [VMEM] * 5,
        [(size,) + plane] * 3,
        mixer=True,
        sems=1,
    )(chunk, c, ra, rb, inv, cc, sinv)[0]
    got = lax.all_to_all(sent.reshape(NSP, 3 * CHUNK, LANES), "space", 0, 0)
    fine, residual = call(finish_kernel, [(2, LANES, 1024), (LANES, 1024)], [VMEM])(got)
    return fine.reshape(1, 2, 4, 32, 1024), residual.reshape(1, 4, 32, 1024)


def solution(mesh):
    inner = Mesh(mesh.devices.reshape(NZD, 2, NSP), ("z", "core", "space"))
    tm = ("z", "core")
    return jax.shard_map(
        body,
        mesh=inner,
        in_specs=(P(tm, "space", None, None), P("space", None, None), P("space", None, None)),
        out_specs=(P(tm, None, "space", None, None), P(tm, "space", None, None)),
        check_vma=False,
    )
```

```python
import functools

import jax
import jax.numpy as jnp
from jax import lax
from jax.experimental import pallas as pl
from jax.experimental.pallas import tpu as pltpu
from jax.sharding import Mesh, PartitionSpec as P

SWEEPS = 4
NT = 16
HALO = 16
CHUNK = 64
WIDE = CHUNK + 2 * HALO
PIECE = 8
STRIP = 4
NZD = 8
NSP = 16
LANES = 128
F32 = jnp.float32

VMEM = pl.BlockSpec(memory_space=pltpu.VMEM)
LIMIT = 16 * 1024 * 1024
MOST = 60 * 1024 * 1024
BF16 = jnp.bfloat16


def call(kernel, out, specs, scratch=(), mixer=False, sems=0, limit=LIMIT):
    outs = [jax.ShapeDtypeStruct(s, F32) for s in out]
    scratch = [pltpu.VMEM(s, F32) for s in scratch]
    if mixer:
        scratch.append(pltpu.VMEM((2 * LANES, 2 * LANES), BF16))
    if sems:
        scratch.append(pltpu.SemaphoreType.DMA((sems,)))
    return pl.pallas_call(
        kernel,
        out_shape=outs,
        in_specs=specs,
        out_specs=[VMEM] * len(out),
        scratch_shapes=scratch,
        compiler_params=pltpu.CompilerParams(vmem_limit_bytes=limit),
    )


SNAKE = [x * 4 + (y if x % 2 == 0 else 3 - y) for x in range(4) for y in range(4)]


def position():
    z, core = lax.axis_index("z"), lax.axis_index("core")
    j = lax.axis_index("space")
    x = j // 4
    odd = x % 2
    y = j % 4
    odd_chunk = (y + odd) % 2
    sub = z + odd_chunk * (NZD - 1 - 2 * z)
    return z, core, odd_chunk, sub


def at_ends():
    j = lax.axis_index("space")
    return j == SNAKE[0], j == SNAKE[-1]


def flat(z, core, j):
    return (z * 2 + core) * NSP + j


def piece_pairs(first):
    path = [
        (z, SNAKE[k])
        for k in range(NSP)
        for z in (range(NZD) if k % 2 == 0 else range(NZD - 1, -1, -1))
    ]
    pairs = []
    for core in (0, 1):
        for q in range(first, len(path), 2):
            (z, j), (other_z, other_j) = path[q], path[(q + 1) % len(path)]
            a, b = flat(z, core, j), flat(other_z, core, other_j)
            pairs += [(a, b), (b, a)]
    return pairs


def chunk_pairs(first):
    pairs = []
    for k in range(first, NSP, 2):
        a, b = SNAKE[k], SNAKE[(k + 1) % NSP]
        pairs += [(a, b), (b, a)]
    return pairs


def interval_shift(step):
    moves = []
    for t in range(NT):
        to = (t + step) % NT
        moves += [(flat(t // 2, t % 2, j), flat(to // 2, to % 2, j)) for j in range(NSP)]
    return moves


def edges(rows):
    shape = (1, rows, LANES)
    lane = lax.broadcasted_iota(jnp.int32, shape, 2)
    row = lax.broadcasted_iota(jnp.int32, shape, 1)
    top, bottom = (lane >= 96) & (row < 15), (lane < 32) & (row > 0)
    return (lane & 31) < 31, (lane & 31) > 0, lane >= 96, lane < 32, top, bottom


def rolled(v):
    z_top, z_bottom, x_top, x_bottom, top, bottom = edges(16)
    total = jnp.where(z_top, pltpu.roll(v, LANES - 1, 2), 0.0)
    total = total + jnp.where(z_bottom, pltpu.roll(v, 1, 2), 0.0)
    up = pltpu.roll(v, LANES - 32, 2)
    down = pltpu.roll(v, 32, 2)
    far_up = jnp.where(top, pltpu.roll(up, 15, 1), 0.0)
    far_down = jnp.where(bottom, pltpu.roll(down, 1, 1), 0.0)
    return total + jnp.where(x_top, far_up, up) + jnp.where(x_bottom, far_down, down)


def fill_mixer(m_ref):
    shape = (2 * LANES, 2 * LANES)
    source = lax.broadcasted_iota(jnp.int32, shape, 0) & (LANES - 1)
    column = lax.broadcasted_iota(jnp.int32, shape, 1)
    lane = column & (LANES - 1)
    apart = jnp.abs(source - lane)
    near = ((apart == 1) & ((source >> 5) == (lane >> 5))) | (apart == 32)
    far = apart == 96
    picked = jnp.where(column < LANES, jnp.where(near, 1.0, 0.0), jnp.where(far, 1.0, 0.0))
    m_ref[...] = picked.astype(BF16)


def mixed(v, m_ref):
    n = v.shape[0]
    _, _, _, _, top, bottom = edges(16)
    x = v.reshape(n * 16, LANES)
    high = x.astype(BF16)
    rest = x - high.astype(F32)
    middle = rest.astype(BF16)
    low = (rest - middle.astype(F32)).astype(BF16)
    both = jnp.concatenate([high, middle], 1)
    p = jnp.dot(both, m_ref[...], preferred_element_type=F32)
    p = p + jnp.dot(low, m_ref[:LANES], preferred_element_type=F32)
    near = p[:, :LANES].reshape(v.shape)
    far = p[:, LANES:].reshape(v.shape)
    across = jnp.where(bottom, pltpu.roll(far, 1, 1), 0.0)
    return near + jnp.where(top, pltpu.roll(far, 15, 1), across)


def lateral(v, m_ref):
    if m_ref is None:
        return rolled(v)
    cut = v.shape[0] // 3
    return jnp.concatenate([rolled(v[:cut]), mixed(v[cut:], m_ref)], 0)


def swept(v, bb, cc, m_ref=None):
    return bb + cc * (lateral(v[1:-1], m_ref) + v[2:] + v[:-2])


def prep_kernel(c_ref, s_ref, r_ref, o_ref, v_ref, q_ref, sems):
    core = lax.axis_index("core")
    zero = jnp.zeros((HALO, LANES), F32)

    def copies(ref, to, first):
        return [
            pltpu.make_async_copy(
                ref.at[:, pl.ds(m * LANES, LANES)], to.at[:, pl.ds(m * LANES, LANES)], sems.at[first + m]
            )
            for m in range(8)
        ]

    def spread(arriving, ref, base):
        for m in range(8):
            arriving[m].wait()
            tile = ref[:, m * LANES : (m + 1) * LANES].T
            for half in range(2):
                k = 2 * m + half
                part = tile[half * 64 : half * 64 + 64]
                o_ref[SNAKE[k], base + HALO : base + HALO + CHUNK] = part
                if k > 0:
                    o_ref[SNAKE[k - 1], base + HALO + CHUNK : base + WIDE] = part[:HALO]
                if k < NSP - 1:
                    o_ref[SNAKE[k + 1], base : base + HALO] = part[CHUNK - HALO :]
        o_ref[SNAKE[0], base : base + HALO] = zero
        o_ref[SNAKE[NSP - 1], base + HALO + CHUNK : base + WIDE] = zero

    states = copies(c_ref, v_ref, 0)
    for copy in states:
        copy.start()

    @pl.when(core == 0)
    def _():
        fields = copies(s_ref, q_ref, 8)
        for copy in fields:
            copy.start()
        spread(fields, q_ref, WIDE)

    @pl.when(core != 0)
    def _():
        fields = copies(r_ref, q_ref, 8)
        for copy in fields:
            copy.start()
        spread(fields, q_ref, WIDE)

    spread(states, v_ref, 0)


def unpack_kernel(a_ref, q_ref):
    def one(y, _):
        q_ref[y] = a_ref[pl.ds(WIDE + y, NSP, stride=2 * WIDE), :]
        return 0

    lax.fori_loop(0, WIDE, one, 0, unroll=8)


def double_step(number, a_ref, b_ref, bb_ref, inv_ref, cc_ref, sinv_ref, m_ref):
    refs = [a_ref, b_ref]
    for step in (number, number + 1):
        edge = step * SWEEPS
        bb_ref[edge : WIDE - edge] = (
            a_ref[edge : WIDE - edge] * inv_ref[edge : WIDE - edge] + sinv_ref[edge : WIDE - edge]
        )
        for sweep in range(SWEEPS):
            src, dst = refs[sweep % 2], refs[(sweep + 1) % 2]
            low = edge + sweep + 1
            high = WIDE - low
            dst[low:high] = swept(src[low - 1 : high + 1], bb_ref[low:high], cc_ref[low:high], m_ref)


def first_kernel(
    g_ref, own_ref, oth_ref, a_ref, u_ref, inv2_ref, cc2_ref, inv_ref, cc_ref, sinv_ref, c_ref,
    b_ref, bb_ref, rate_ref, m_ref,
):
    _, core, _, sub = position()
    step = 8
    fill_mixer(m_ref)

    def gather(y, _):
        a_ref[y] = g_ref[pl.ds(y, NSP, stride=2 * WIDE), :]
        return 0

    lax.fori_loop(0, WIDE, gather, 0, unroll=8)
    c_ref[...] = a_ref[HALO : HALO + CHUNK]

    def init(n, _):
        at = pl.ds(pl.multiple_of(n * step, step), step)
        own, oth = own_ref[at], oth_ref[at]
        source = jnp.where(core == 0, own, oth)
        rate = jnp.where(core == 0, oth, own)
        inv = 1.0 / (1.0 + 6.0 * rate)
        rate_ref[at] = rate
        inv_ref[at] = inv
        cc_ref[at] = rate * inv
        sinv_ref[at] = source * inv
        return 0

    lax.fori_loop(0, WIDE // step, init, 0)
    double_step(0, a_ref, b_ref, bb_ref, inv_ref, cc_ref, sinv_ref, m_ref)
    u_ref[...] = a_ref[HALO : HALO + CHUNK]
    rate = 2.0 * rate_ref[pl.ds(HALO - PIECE + PIECE * sub, 3 * PIECE)]
    inv = 1.0 / (1.0 + 6.0 * rate)
    inv2_ref[...] = inv
    cc2_ref[...] = rate * inv


def second_kernel(u_ref, inv_ref, cc_ref, sinv_ref, w_ref, a_ref, b_ref, bb_ref, m_ref):
    fill_mixer(m_ref)
    a_ref[...] = u_ref[...]
    double_step(2, a_ref, b_ref, bb_ref, inv_ref, cc_ref, sinv_ref, m_ref)
    w_ref[...] = a_ref[HALO : HALO + CHUNK]


def difference_kernel(w_ref, next_ref, r_ref, low_ref, high_ref):
    z, core, odd, _ = position()
    last = (z == NZD - 1) & (core == 1)
    for n in range(NZD):
        part = jnp.where(odd == 1, NZD - 1 - n, n)
        after = next_ref[pl.ds(PIECE * part, PIECE)]
        r = jnp.where(last, after, w_ref[pl.ds(PIECE * part, PIECE)]) - after
        r_ref[n] = r
        half = low_ref if n < NZD // 2 else high_ref
        half[n % (NZD // 2)] = r


def messages(odd, e, r_next, a_ref, b_ref):
    head, tail = r_next[:STRIP], r_next[STRIP:]
    a_ref[:PIECE] = e
    b_ref[:PIECE] = e
    a_ref[PIECE:] = jnp.where(odd == 0, tail, head)
    b_ref[PIECE:] = jnp.where(odd == 0, head, tail)


def residual_kernel(own_ref, oth_ref, r_ref, a_ref, b_ref):
    _, core, _, sub = position()
    for t in range(1, NT):
        n = (t // 2 - 1) % NZD
        r_ref[t] = jnp.where(core == t % 2, own_ref[n], oth_ref[n])
    messages(sub % 2, r_ref[1], r_ref[2], a_ref, b_ref)


def coarse_step(v, inv, cc):
    bb = v * inv
    for sweep in range(SWEEPS):
        low = sweep + 1
        high = bb.shape[0] - low
        v = swept(v, bb[low:high], cc[low:high])
    return v


def chain_step(t, ra_ref, rb_ref, e_ref, r_ref, inv_ref, cc_ref):
    sub = position()[3]
    odd = sub % 2
    bottom, top = at_ends()
    ra, rb = ra_ref[...], rb_ref[...]
    left = jnp.where(bottom & (sub == 0), 0.0, jnp.where(odd == 0, rb, ra))
    right = jnp.where(top & (sub == NZD - 1), 0.0, jnp.where(odd == 0, ra, rb))
    e = jnp.concatenate([left[:PIECE], e_ref[...], right[:PIECE]], 0)
    r1 = jnp.concatenate([left[PIECE:], r_ref[t + 1], right[PIECE:]], 0)
    inv, cc = inv_ref[...], cc_ref[...]
    e1 = coarse_step(e, inv, cc) + r1
    e2 = coarse_step(e1, inv[STRIP:-STRIP], cc[STRIP:-STRIP]) + r_ref[t + 2]
    return e1[STRIP:-STRIP], e2


def chain_kernel(t, ra_ref, rb_ref, e_ref, r_ref, inv_ref, cc_ref, e1_ref, e2_ref, a_ref, b_ref):
    sub = position()[3]
    e1, e2 = chain_step(t, ra_ref, rb_ref, e_ref, r_ref, inv_ref, cc_ref)
    e1_ref[...] = e1
    e2_ref[...] = e2
    messages(sub % 2, e2, r_ref[t + 3], a_ref, b_ref)


def chain_end_kernel(t, ra_ref, rb_ref, r_ref, inv_ref, cc_ref, *refs):
    core = lax.axis_index("core")
    e_refs, o_ref = refs[:-1], refs[-1]
    e1, e2 = chain_step(t, ra_ref, rb_ref, e_refs[-1], r_ref, inv_ref, cc_ref)
    errors = [jnp.zeros(e1.shape, F32)] + [ref[...] for ref in e_refs] + [e1, e2]
    for n in range(NT // 2):
        o_ref[n] = jnp.where(core == 0, errors[2 * n], errors[2 * n + 1])


def last_kernel(
    e_ref, cp_ref, low_ref, high_ref, c_ref, ra_ref, rb_ref, inv_ref, cc_ref, sinv_ref, o_ref,
    a_ref, b_ref, bb_ref, m_ref, sems
):
    device_z, core, odd, _ = position()
    first = (device_z == 0) & (core == 0)
    size = CHUNK + 2 * STRIP
    fill_mixer(m_ref)
    for n in range(NZD):
        z = jnp.where(odd == 1, NZD - 1 - n, n)
        at = n * PIECE
        a_ref[STRIP + at : STRIP + at + PIECE] = cp_ref[at : at + PIECE] + e_ref[z]
    for n in range(NZD):
        at = n * PIECE
        for y in range(PIECE):
            half = low_ref if n < NZD // 2 else high_ref
            part = jnp.where(odd == 1, NZD - 1 - n, n)
            row = 2 * CHUNK + part * PIECE + y
            o_ref[pl.ds(row, NSP, stride=3 * CHUNK), :] = jnp.where(first, 0.0, half[n % (NZD // 2), y])
    bottom, top = at_ends()
    a_ref[:STRIP] = jnp.where(bottom, 0.0, jnp.where(odd == 0, rb_ref[...], ra_ref[...]))
    a_ref[STRIP + CHUNK : size] = jnp.where(top, 0.0, jnp.where(odd == 0, ra_ref[...], rb_ref[...]))

    @pl.when(first)
    def _():
        copy = pltpu.make_async_copy(c_ref, a_ref.at[pl.ds(STRIP, CHUNK)], sems.at[0])
        copy.start()
        copy.wait()

    off = HALO - STRIP
    bb_ref[...] = a_ref[...] * inv_ref[off : off + size] + sinv_ref[off : off + size]

    def keep(which):
        def one(y, _):
            o_ref[pl.ds(which * CHUNK + y, NSP, stride=3 * CHUNK), :] = a_ref[STRIP + y]
            return 0

        lax.fori_loop(0, CHUNK, one, 0, unroll=8)

    keep(0)
    refs = [a_ref, b_ref]
    for sweep in range(SWEEPS):
        src, dst = refs[sweep % 2], refs[(sweep + 1) % 2]
        low = sweep + 1
        high = size - low
        dst[low:high] = swept(
            src[low - 1 : high + 1], bb_ref[low:high], cc_ref[off + low : off + high], m_ref
        )
    keep(1)


def finish_kernel(a_ref, f_ref, r_ref):
    outs = [f_ref.at[0], f_ref.at[1], r_ref]
    for which in range(3):
        for m in range(8):
            low = a_ref[SNAKE[2 * m], which * CHUNK : (which + 1) * CHUNK]
            high = a_ref[SNAKE[2 * m + 1], which * CHUNK : (which + 1) * CHUNK]
            outs[which][:, m * 128 : (m + 1) * 128] = jnp.concatenate([low, high], 0).T


def strips_kernel(e_ref, cp_ref, c_ref, a_ref, b_ref, head_ref, tail_ref, sems):
    z, core, odd, _ = position()
    low, high = odd * (NZD - 1), (1 - odd) * (NZD - 1)
    head_ref[...] = cp_ref[:STRIP] + e_ref[low, :STRIP]
    tail_ref[...] = cp_ref[CHUNK - STRIP :] + e_ref[high, STRIP:]

    @pl.when((z == 0) & (core == 0))
    def _():
        copies = [
            pltpu.make_async_copy(c_ref.at[pl.ds(0, STRIP)], head_ref, sems.at[0]),
            pltpu.make_async_copy(c_ref.at[pl.ds(CHUNK - STRIP, STRIP)], tail_ref, sems.at[1]),
        ]
        for copy in copies:
            copy.start()
        for copy in copies:
            copy.wait()

    head, tail = head_ref[...], tail_ref[...]
    a_ref[...] = jnp.where(odd == 0, tail, head)
    b_ref[...] = jnp.where(odd == 0, head, tail)


def body(c_guess, source, rate):
    everyone = ("z", "core", "space")
    anywhere = pl.BlockSpec(memory_space=pltpu.HBM)
    plane = (16, LANES)
    piece = (PIECE,) + plane
    message = (PIECE + STRIP,) + plane

    def swap(v):
        return lax.ppermute(v, "core", [(0, 1), (1, 0)])

    sent = call(
        prep_kernel, [(NSP, 2 * WIDE, LANES)], [anywhere] * 3, [(LANES, 1024)] * 2, sems=16, limit=MOST
    )(c_guess.reshape(LANES, -1), source.reshape(LANES, -1), rate.reshape(LANES, -1))[0]
    got = lax.all_to_all(sent, "space", 0, 0).reshape(-1, LANES)
    own = call(unpack_kernel, [(WIDE,) + plane], [VMEM])(got)[0]
    oth = swap(own)

    wide, whole = (WIDE,) + plane, (CHUNK,) + plane
    ahead, u, inv2, cc2, inv, cc, sinv, c = call(
        first_kernel,
        [wide, whole] + [(3 * PIECE,) + plane] * 2 + [wide] * 3 + [whole],
        [VMEM] * 3,
        [wide] * 3,
        mixer=True,
    )(got, own, oth)
    after = lax.ppermute(u, everyone, interval_shift(-1))
    w = call(second_kernel, [whole], [VMEM] * 4, [wide] * 3, mixer=True)(ahead, inv, cc, sinv)[0]
    half = (NZD // 2,) + piece
    r, r_low, r_high = call(difference_kernel, [(NZD,) + piece, half, half], [VMEM] * 2)(w, after)

    mine = lax.all_to_all(r, "z", 0, 0)
    other = swap(mine)
    res, ma, mb = call(
        residual_kernel, [(NT,) + piece, message, message], [VMEM] * 2
    )(mine, other)
    pairs_a, pairs_b = piece_pairs(0), piece_pairs(1)
    beside = {0: (u, 1), 2: (r_low, 2), 4: (r_high, 2)}
    moved = []
    errors = [res[1]]
    for turn in range(7):
        t = 2 * turn + 1
        ra = lax.ppermute(ma, everyone, pairs_a)
        rb = lax.ppermute(mb, everyone, pairs_b)
        if turn in beside:
            part, step = beside[turn]
            ra, rb, part = lax.optimization_barrier((ra, rb, part))
            moved.append(lax.ppermute(part, everyone, interval_shift(step)))
        if turn == 6:
            break
        e1, e2, ma, mb = call(
            functools.partial(chain_kernel, t), [piece, piece, message, message], [VMEM] * 6
        )(ra, rb, errors[-1], res, inv2, cc2)
        errors += [e1, e2]
        if turn - 1 in beside:
            ma, moved[-1] = lax.optimization_barrier((ma, moved[-1]))
    cpoint, low, high = moved
    errors = call(
        functools.partial(chain_end_kernel, NT - 3),
        [(NZD,) + piece],
        [VMEM] * (5 + len(errors)),
    )(ra, rb, res, inv2, cc2, *errors)[0]

    chunk = lax.all_to_all(errors, "z", 0, 0)
    edge = (STRIP,) + plane
    ma, mb = call(strips_kernel, [edge] * 2, [VMEM] * 2 + [anywhere], [edge] * 2, sems=2)(
        chunk, cpoint, c
    )
    ra = lax.ppermute(ma, "space", chunk_pairs(0))
    rb = lax.ppermute(mb, "space", chunk_pairs(1))
    sent = call(
        last_kernel,
        [(NSP * 3 * CHUNK, LANES)],
        [VMEM] * 4 + [anywhere] + [VMEM] * 5,
        [(CHUNK + 2 * STRIP,) + plane] * 3,
        mixer=True,
        sems=1,
    )(chunk, cpoint, low, high, c, ra, rb, inv, cc, sinv)[0]
    got = lax.all_to_all(sent.reshape(NSP, 3 * CHUNK, LANES), "space", 0, 0)
    fine, residual = call(finish_kernel, [(2, LANES, 1024), (LANES, 1024)], [VMEM])(got)
    return fine.reshape(1, 2, 4, 32, 1024), residual.reshape(1, 4, 32, 1024)


def solution(mesh):
    inner = Mesh(mesh.devices.reshape(NZD, 2, NSP), ("z", "core", "space"))
    tm = ("z", "core")
    return jax.shard_map(
        body,
        mesh=inner,
        in_specs=(P(tm, "space", None, None), P("space", None, None), P("space", None, None)),
        out_specs=(P(tm, None, "space", None, None), P(tm, "space", None, None)),
        check_vma=False,
    )
```

```python
import functools

import jax
import jax.numpy as jnp
from jax import lax
from jax.experimental import pallas as pl
from jax.experimental.pallas import tpu as pltpu
from jax.sharding import Mesh, PartitionSpec as P

SWEEPS = 4
NT = 16
HALO = 16
CHUNK = 64
WIDE = CHUNK + 2 * HALO
PIECE = 8
STRIP = 4
NZD = 8
NSP = 16
LANES = 128
BLOCK = 32
F32 = jnp.float32

VMEM = pl.BlockSpec(memory_space=pltpu.VMEM)
LIMIT = 16 * 1024 * 1024
MOST = 60 * 1024 * 1024
BF16 = jnp.bfloat16


def call(kernel, out, specs, scratch=(), mixer=False, sems=(), limit=LIMIT, aliases=None, to=VMEM):
    outs = [jax.ShapeDtypeStruct(s, F32) for s in out]
    scratch = [pltpu.VMEM(s, F32) for s in scratch]
    if mixer:
        scratch.append(pltpu.VMEM((2 * LANES, 2 * LANES), BF16))
    for count in sems:
        scratch.append(pltpu.SemaphoreType.DMA(count))
    return pl.pallas_call(
        kernel,
        out_shape=outs,
        in_specs=specs,
        out_specs=[to] * len(out),
        input_output_aliases=aliases or {},
        scratch_shapes=scratch,
        compiler_params=pltpu.CompilerParams(vmem_limit_bytes=limit),
    )


SNAKE = [x * 4 + (y if x % 2 == 0 else 3 - y) for x in range(4) for y in range(4)]


def position():
    z, core = lax.axis_index("z"), lax.axis_index("core")
    j = lax.axis_index("space")
    x = j // 4
    odd = x % 2
    y = j % 4
    odd_chunk = (y + odd) % 2
    sub = z + odd_chunk * (NZD - 1 - 2 * z)
    return z, core, odd_chunk, sub


def at_ends():
    j = lax.axis_index("space")
    return j == SNAKE[0], j == SNAKE[-1]


def flat(z, core, j):
    return (z * 2 + core) * NSP + j


def piece_pairs(first):
    path = [
        (z, SNAKE[k])
        for k in range(NSP)
        for z in (range(NZD) if k % 2 == 0 else range(NZD - 1, -1, -1))
    ]
    pairs = []
    for core in (0, 1):
        for q in range(first, len(path), 2):
            (z, j), (other_z, other_j) = path[q], path[(q + 1) % len(path)]
            a, b = flat(z, core, j), flat(other_z, core, other_j)
            pairs += [(a, b), (b, a)]
    return pairs


def chunk_pairs(first):
    pairs = []
    for k in range(first, NSP, 2):
        a, b = SNAKE[k], SNAKE[(k + 1) % NSP]
        pairs += [(a, b), (b, a)]
    return pairs


def interval_shift(step):
    moves = []
    for t in range(NT):
        to = (t + step) % NT
        moves += [(flat(t // 2, t % 2, j), flat(to // 2, to % 2, j)) for j in range(NSP)]
    return moves


def edges(rows):
    shape = (1, rows, LANES)
    lane = lax.broadcasted_iota(jnp.int32, shape, 2)
    row = lax.broadcasted_iota(jnp.int32, shape, 1)
    top, bottom = (lane >= 96) & (row < 15), (lane < 32) & (row > 0)
    return (lane & 31) < 31, (lane & 31) > 0, lane >= 96, lane < 32, top, bottom


def rolled(v):
    z_top, z_bottom, x_top, x_bottom, top, bottom = edges(16)
    total = jnp.where(z_top, pltpu.roll(v, LANES - 1, 2), 0.0)
    total = total + jnp.where(z_bottom, pltpu.roll(v, 1, 2), 0.0)
    up = pltpu.roll(v, LANES - 32, 2)
    down = pltpu.roll(v, 32, 2)
    far_up = jnp.where(top, pltpu.roll(up, 15, 1), 0.0)
    far_down = jnp.where(bottom, pltpu.roll(down, 1, 1), 0.0)
    return total + jnp.where(x_top, far_up, up) + jnp.where(x_bottom, far_down, down)


def fill_mixer(m_ref):
    shape = (2 * LANES, 2 * LANES)
    source = lax.broadcasted_iota(jnp.int32, shape, 0) & (LANES - 1)
    column = lax.broadcasted_iota(jnp.int32, shape, 1)
    lane = column & (LANES - 1)
    apart = jnp.abs(source - lane)
    near = ((apart == 1) & ((source >> 5) == (lane >> 5))) | (apart == 32)
    far = apart == 96
    picked = jnp.where(column < LANES, jnp.where(near, 1.0, 0.0), jnp.where(far, 1.0, 0.0))
    m_ref[...] = picked.astype(BF16)


def mixed(v, m_ref):
    n = v.shape[0]
    _, _, _, _, top, bottom = edges(16)
    x = v.reshape(n * 16, LANES)
    high = x.astype(BF16)
    rest = x - high.astype(F32)
    middle = rest.astype(BF16)
    low = (rest - middle.astype(F32)).astype(BF16)
    both = jnp.concatenate([high, middle], 1)
    p = jnp.dot(both, m_ref[...], preferred_element_type=F32)
    p = p + jnp.dot(low, m_ref[:LANES], preferred_element_type=F32)
    near = p[:, :LANES].reshape(v.shape)
    far = p[:, LANES:].reshape(v.shape)
    across = jnp.where(bottom, pltpu.roll(far, 1, 1), 0.0)
    return near + jnp.where(top, pltpu.roll(far, 15, 1), across)


def lateral(v, m_ref):
    if m_ref is None:
        return rolled(v)
    sums = []
    for first in range(0, v.shape[0], BLOCK):
        block = v[first : first + BLOCK]
        cut = block.shape[0] // 4
        if cut > 0:
            sums.append(rolled(block[:cut]))
        sums.append(mixed(block[cut:], m_ref))
    return jnp.concatenate(sums, 0)


def swept(v, bb, cc, m_ref=None):
    return bb + cc * (lateral(v[1:-1], m_ref) + v[2:] + v[:-2])


def prep_kernel(c_ref, s_ref, r_ref, out_ref, v_ref, q_ref, o_ref, sems, out_sems):
    zero = jnp.zeros((HALO, LANES), F32)

    def copies(ref, to, first):
        return [
            pltpu.make_async_copy(
                ref.at[:, pl.ds(m * LANES, LANES)], to.at[:, pl.ds(m * LANES, LANES)], sems.at[first + m]
            )
            for m in range(8)
        ]

    def spread(arriving, ref, base):
        leaving = []

        def send(k):
            rows = pl.ds(base, WIDE)
            leaving.append(
                pltpu.make_async_copy(
                    o_ref.at[SNAKE[k], rows], out_ref.at[SNAKE[k], rows], out_sems.at[base // WIDE, k]
                )
            )
            leaving[-1].start()

        o_ref[SNAKE[0], base : base + HALO] = zero
        o_ref[SNAKE[NSP - 1], base + HALO + CHUNK : base + WIDE] = zero
        for m in range(8):
            arriving[m].wait()
            tile = ref[:, m * LANES : (m + 1) * LANES].T
            for half in range(2):
                k = 2 * m + half
                part = tile[half * 64 : half * 64 + 64]
                o_ref[SNAKE[k], base + HALO : base + HALO + CHUNK] = part
                if k > 0:
                    o_ref[SNAKE[k - 1], base + HALO + CHUNK : base + WIDE] = part[:HALO]
                    send(k - 1)
                if k < NSP - 1:
                    o_ref[SNAKE[k + 1], base : base + HALO] = part[CHUNK - HALO :]
        send(NSP - 1)
        return leaving

    def work(ref):
        states, fields = copies(c_ref, v_ref, 0), copies(ref, q_ref, 8)
        for copy in states + fields:
            copy.start()
        leaving = spread(states, v_ref, 0) + spread(fields, q_ref, WIDE)
        for copy in leaving:
            copy.wait()

    core = lax.axis_index("core")

    @pl.when(core == 0)
    def _():
        work(s_ref)

    @pl.when(core != 0)
    def _():
        work(r_ref)


def unpack_kernel(a_ref, q_ref):
    def one(y, _):
        q_ref[y] = a_ref[pl.ds(WIDE + y, NSP, stride=2 * WIDE), :]
        return 0

    lax.fori_loop(0, WIDE, one, 0, unroll=8)


def double_step(number, a_ref, b_ref, bb_ref, inv_ref, cc_ref, sinv_ref, m_ref):
    refs = [a_ref, b_ref]
    for step in (number, number + 1):
        edge = step * SWEEPS
        bb_ref[edge : WIDE - edge] = (
            a_ref[edge : WIDE - edge] * inv_ref[edge : WIDE - edge] + sinv_ref[edge : WIDE - edge]
        )
        for sweep in range(SWEEPS):
            src, dst = refs[sweep % 2], refs[(sweep + 1) % 2]
            low = edge + sweep + 1
            high = WIDE - low
            dst[low:high] = swept(src[low - 1 : high + 1], bb_ref[low:high], cc_ref[low:high], m_ref)


def first_kernel(
    g_ref, own_ref, oth_ref, a_ref, u_ref, inv2_ref, cc2_ref, inv_ref, cc_ref, sinv_ref, c_ref,
    b_ref, bb_ref, rate_ref, m_ref,
):
    _, core, _, sub = position()
    step = 8
    fill_mixer(m_ref)

    def gather(y, _):
        a_ref[y] = g_ref[pl.ds(y, NSP, stride=2 * WIDE), :]
        return 0

    lax.fori_loop(0, WIDE, gather, 0, unroll=8)
    c_ref[...] = a_ref[HALO : HALO + CHUNK]

    def init(n, _):
        at = pl.ds(pl.multiple_of(n * step, step), step)
        own, oth = own_ref[at], oth_ref[at]
        source = jnp.where(core == 0, own, oth)
        rate = jnp.where(core == 0, oth, own)
        inv = 1.0 / (1.0 + 6.0 * rate)
        rate_ref[at] = rate
        inv_ref[at] = inv
        cc_ref[at] = rate * inv
        sinv_ref[at] = source * inv
        return 0

    lax.fori_loop(0, WIDE // step, init, 0)
    double_step(0, a_ref, b_ref, bb_ref, inv_ref, cc_ref, sinv_ref, m_ref)
    u_ref[...] = a_ref[HALO : HALO + CHUNK]
    rate = 2.0 * rate_ref[pl.ds(HALO - PIECE + PIECE * sub, 3 * PIECE)]
    inv = 1.0 / (1.0 + 6.0 * rate)
    inv2_ref[...] = inv
    cc2_ref[...] = rate * inv


def second_kernel(u_ref, inv_ref, cc_ref, sinv_ref, w_ref, a_ref, b_ref, bb_ref, m_ref):
    fill_mixer(m_ref)
    a_ref[...] = u_ref[...]
    double_step(2, a_ref, b_ref, bb_ref, inv_ref, cc_ref, sinv_ref, m_ref)
    w_ref[...] = a_ref[HALO : HALO + CHUNK]


def difference_kernel(w_ref, next_ref, r_ref, low_ref, high_ref):
    z, core, odd, _ = position()
    last = (z == NZD - 1) & (core == 1)
    for n in range(NZD):
        part = jnp.where(odd == 1, NZD - 1 - n, n)
        after = next_ref[pl.ds(PIECE * part, PIECE)]
        r = jnp.where(last, after, w_ref[pl.ds(PIECE * part, PIECE)]) - after
        r_ref[n] = r
        half = low_ref if n < NZD // 2 else high_ref
        half[n % (NZD // 2)] = r


def messages(odd, e, r_next, a_ref, b_ref):
    head, tail = r_next[:STRIP], r_next[STRIP:]
    a_ref[:PIECE] = e
    b_ref[:PIECE] = e
    a_ref[PIECE:] = jnp.where(odd == 0, tail, head)
    b_ref[PIECE:] = jnp.where(odd == 0, head, tail)


def residual_kernel(own_ref, oth_ref, r_ref, a_ref, b_ref):
    _, core, _, sub = position()
    for t in range(1, NT):
        n = (t // 2 - 1) % NZD
        r_ref[t] = jnp.where(core == t % 2, own_ref[n], oth_ref[n])
    messages(sub % 2, r_ref[1], r_ref[2], a_ref, b_ref)


def coarse_step(v, inv, cc):
    bb = v * inv
    for sweep in range(SWEEPS):
        low = sweep + 1
        high = bb.shape[0] - low
        v = swept(v, bb[low:high], cc[low:high])
    return v


def chain_step(t, ra_ref, rb_ref, e_ref, r_ref, inv_ref, cc_ref):
    sub = position()[3]
    odd = sub % 2
    bottom, top = at_ends()
    ra, rb = ra_ref[...], rb_ref[...]
    left = jnp.where(bottom & (sub == 0), 0.0, jnp.where(odd == 0, rb, ra))
    right = jnp.where(top & (sub == NZD - 1), 0.0, jnp.where(odd == 0, ra, rb))
    e = jnp.concatenate([left[:PIECE], e_ref[...], right[:PIECE]], 0)
    r1 = jnp.concatenate([left[PIECE:], r_ref[t + 1], right[PIECE:]], 0)
    inv, cc = inv_ref[...], cc_ref[...]
    e1 = coarse_step(e, inv, cc) + r1
    e2 = coarse_step(e1, inv[STRIP:-STRIP], cc[STRIP:-STRIP]) + r_ref[t + 2]
    return e1[STRIP:-STRIP], e2


def chain_kernel(t, ra_ref, rb_ref, e_ref, r_ref, inv_ref, cc_ref, e1_ref, e2_ref, a_ref, b_ref):
    sub = position()[3]
    e1, e2 = chain_step(t, ra_ref, rb_ref, e_ref, r_ref, inv_ref, cc_ref)
    e1_ref[...] = e1
    e2_ref[...] = e2
    messages(sub % 2, e2, r_ref[t + 3], a_ref, b_ref)


def chain_end_kernel(t, ra_ref, rb_ref, r_ref, inv_ref, cc_ref, *refs):
    core = lax.axis_index("core")
    e_refs, o_ref = refs[:-1], refs[-1]
    e1, e2 = chain_step(t, ra_ref, rb_ref, e_refs[-1], r_ref, inv_ref, cc_ref)
    errors = [jnp.zeros(e1.shape, F32)] + [ref[...] for ref in e_refs] + [e1, e2]
    for n in range(NT // 2):
        o_ref[n] = jnp.where(core == 0, errors[2 * n], errors[2 * n + 1])


def keep(o_ref, which, values_ref, low, high):
    def one(y, _):
        o_ref[pl.ds(which * CHUNK + y, NSP, stride=3 * CHUNK), :] = values_ref[y]
        return 0

    lax.fori_loop(low, high, one, 0, unroll=8)


def inner_kernel(
    e_ref, cp_ref, low_ref, high_ref, c_ref, inv_ref, cc_ref, sinv_ref, o_ref, edge_ref,
    a_ref, b_ref, bb_ref, m_ref, sems
):
    z, core, odd, _ = position()
    first = (z == 0) & (core == 0)
    fill_mixer(m_ref)
    for n in range(NZD):
        at = n * PIECE
        a_ref[at : at + PIECE] = cp_ref[at : at + PIECE] + e_ref[jnp.where(odd == 1, NZD - 1 - n, n)]

    @pl.when(first)
    def _():
        copy = pltpu.make_async_copy(c_ref, a_ref, sems.at[0])
        copy.start()
        copy.wait()

    bb_ref[...] = a_ref[...] * inv_ref[HALO : HALO + CHUNK] + sinv_ref[HALO : HALO + CHUNK]
    edge_ref[0] = a_ref[: 2 * STRIP]
    edge_ref[1] = a_ref[CHUNK - 2 * STRIP :]
    keep(o_ref, 0, a_ref, 0, CHUNK)
    refs = [a_ref, b_ref]
    for sweep in range(SWEEPS):
        src, dst = refs[sweep % 2], refs[(sweep + 1) % 2]
        low = sweep + 1
        high = CHUNK - low
        dst[low:high] = swept(
            src[low - 1 : high + 1], bb_ref[low:high], cc_ref[HALO + low : HALO + high], m_ref
        )
    keep(o_ref, 1, a_ref, STRIP, CHUNK - STRIP)
    for n in range(NZD):
        half = low_ref if n < NZD // 2 else high_ref
        part = jnp.where(odd == 1, NZD - 1 - n, n)
        for y in range(PIECE):
            row = 2 * CHUNK + part * PIECE + y
            o_ref[pl.ds(row, NSP, stride=3 * CHUNK), :] = jnp.where(first, 0.0, half[n % (NZD // 2), y])


def outer_kernel(s_ref, edge_ref, ra_ref, rb_ref, inv_ref, cc_ref, sinv_ref, o_ref):
    odd = position()[2]
    bottom, top = at_ends()
    before = jnp.where(bottom, 0.0, jnp.where(odd == 0, rb_ref[...], ra_ref[...]))
    behind = jnp.where(top, 0.0, jnp.where(odd == 0, ra_ref[...], rb_ref[...]))
    v = jnp.concatenate([before, edge_ref[0], edge_ref[1], behind], 0)

    def both(ref):
        start, end = HALO - STRIP, HALO + CHUNK + STRIP
        return jnp.concatenate([ref[start : start + 3 * STRIP], ref[end - 3 * STRIP : end]], 0)

    bb, cc = v * both(inv_ref) + both(sinv_ref), both(cc_ref)
    size = v.shape[0]
    for sweep in range(SWEEPS):
        low = sweep + 1
        v = swept(v, bb[low : size - low], cc[low : size - low])
    for y in range(STRIP):
        o_ref[pl.ds(CHUNK + y, NSP, stride=3 * CHUNK), :] = v[y]
        row = 2 * CHUNK - STRIP + y
        o_ref[pl.ds(row, NSP, stride=3 * CHUNK), :] = v[v.shape[0] - STRIP + y]


def finish_kernel(a_ref, f_ref, r_ref, v_ref, sems):
    copies = []
    for which, to in enumerate((f_ref.at[0], f_ref.at[1], r_ref)):
        for m in range(8):
            low = a_ref[SNAKE[2 * m], which * CHUNK : (which + 1) * CHUNK]
            high = a_ref[SNAKE[2 * m + 1], which * CHUNK : (which + 1) * CHUNK]
            v_ref[which, :, m * LANES : (m + 1) * LANES] = jnp.concatenate([low, high], 0).T
        copies.append(pltpu.make_async_copy(v_ref.at[which], to, sems.at[which]))
        copies[-1].start()
    for copy in copies:
        copy.wait()


def strips_kernel(e_ref, cp_ref, c_ref, a_ref, b_ref, head_ref, tail_ref, sems):
    z, core, odd, _ = position()
    low, high = odd * (NZD - 1), (1 - odd) * (NZD - 1)
    head_ref[...] = cp_ref[:STRIP] + e_ref[low, :STRIP]
    tail_ref[...] = cp_ref[CHUNK - STRIP :] + e_ref[high, STRIP:]

    @pl.when((z == 0) & (core == 0))
    def _():
        copies = [
            pltpu.make_async_copy(c_ref.at[pl.ds(0, STRIP)], head_ref, sems.at[0]),
            pltpu.make_async_copy(c_ref.at[pl.ds(CHUNK - STRIP, STRIP)], tail_ref, sems.at[1]),
        ]
        for copy in copies:
            copy.start()
        for copy in copies:
            copy.wait()

    head, tail = head_ref[...], tail_ref[...]
    a_ref[...] = jnp.where(odd == 0, tail, head)
    b_ref[...] = jnp.where(odd == 0, head, tail)


def body(c_guess, source, rate):
    everyone = ("z", "core", "space")
    anywhere = pl.BlockSpec(memory_space=pltpu.HBM)
    plane = (16, LANES)
    piece = (PIECE,) + plane
    message = (PIECE + STRIP,) + plane

    def swap(v):
        return lax.ppermute(v, "core", [(0, 1), (1, 0)])

    sent = call(
        prep_kernel, [(NSP, 2 * WIDE, LANES)], [anywhere] * 3, [(LANES, 1024)] * 2 + [(NSP, 2 * WIDE, LANES)], sems=((16,), (2, NSP)), limit=MOST, to=anywhere
    )(c_guess.reshape(LANES, -1), source.reshape(LANES, -1), rate.reshape(LANES, -1))[0]
    got = lax.all_to_all(sent, "space", 0, 0).reshape(-1, LANES)
    own = call(unpack_kernel, [(WIDE,) + plane], [VMEM])(got)[0]
    oth = swap(own)

    wide, whole = (WIDE,) + plane, (CHUNK,) + plane
    ahead, u, inv2, cc2, inv, cc, sinv, c = call(
        first_kernel,
        [wide, whole] + [(3 * PIECE,) + plane] * 2 + [wide] * 3 + [whole],
        [VMEM] * 3,
        [wide] * 3,
        mixer=True,
    )(got, own, oth)
    after = lax.ppermute(u, everyone, interval_shift(-1))
    w = call(second_kernel, [whole], [VMEM] * 4, [wide] * 3, mixer=True)(ahead, inv, cc, sinv)[0]
    half = (NZD // 2,) + piece
    r, r_low, r_high = call(difference_kernel, [(NZD,) + piece, half, half], [VMEM] * 2)(w, after)

    mine = lax.all_to_all(r, "z", 0, 0)
    other = swap(mine)
    res, ma, mb = call(
        residual_kernel, [(NT,) + piece, message, message], [VMEM] * 2
    )(mine, other)
    pairs_a, pairs_b = piece_pairs(0), piece_pairs(1)
    beside = {0: (u, 1), 2: (r_low, 2), 4: (r_high, 2)}
    moved = []
    errors = [res[1]]
    for turn in range(7):
        t = 2 * turn + 1
        ra = lax.ppermute(ma, everyone, pairs_a)
        rb = lax.ppermute(mb, everyone, pairs_b)
        if turn in beside:
            part, step = beside[turn]
            ra, rb, part = lax.optimization_barrier((ra, rb, part))
            moved.append(lax.ppermute(part, everyone, interval_shift(step)))
        if turn == 6:
            break
        e1, e2, ma, mb = call(
            functools.partial(chain_kernel, t), [piece, piece, message, message], [VMEM] * 6
        )(ra, rb, errors[-1], res, inv2, cc2)
        errors += [e1, e2]
        if turn - 1 in beside:
            ma, moved[-1] = lax.optimization_barrier((ma, moved[-1]))
    cpoint, low, high = moved
    errors = call(
        functools.partial(chain_end_kernel, NT - 3),
        [(NZD,) + piece],
        [VMEM] * (5 + len(errors)),
    )(ra, rb, res, inv2, cc2, *errors)[0]

    chunk = lax.all_to_all(errors, "z", 0, 0)
    edge = (STRIP,) + plane
    ma, mb = call(strips_kernel, [edge] * 2, [VMEM] * 2 + [anywhere], [edge] * 2, sems=((2,),))(
        chunk, cpoint, c
    )
    ra = lax.ppermute(ma, "space", chunk_pairs(0))
    rb = lax.ppermute(mb, "space", chunk_pairs(1))
    sent, edges_in = call(
        inner_kernel,
        [(NSP * 3 * CHUNK, LANES), (2, 2 * STRIP) + plane],
        [VMEM] * 4 + [anywhere] + [VMEM] * 3,
        [whole] * 3,
        mixer=True,
        sems=((1,),),
    )(chunk, cpoint, low, high, c, inv, cc, sinv)
    sent = call(outer_kernel, [(NSP * 3 * CHUNK, LANES)], [VMEM] * 7, aliases={0: 0})(
        sent, edges_in, ra, rb, inv, cc, sinv
    )[0]
    got = lax.all_to_all(sent.reshape(NSP, 3 * CHUNK, LANES), "space", 0, 0)
    fine, residual = call(
        finish_kernel,
        [(2, LANES, 1024), (LANES, 1024)],
        [VMEM],
        [(3, LANES, 1024)],
        sems=((3,),),
        to=anywhere,
    )(got)
    return fine.reshape(1, 2, 4, 32, 1024), residual.reshape(1, 4, 32, 1024)


def solution(mesh):
    inner = Mesh(mesh.devices.reshape(NZD, 2, NSP), ("z", "core", "space"))
    tm = ("z", "core")
    return jax.shard_map(
        body,
        mesh=inner,
        in_specs=(P(tm, "space", None, None), P("space", None, None), P("space", None, None)),
        out_specs=(P(tm, None, "space", None, None), P(tm, "space", None, None)),
        check_vma=False,
    )
```

```python
import functools

import jax
import jax.numpy as jnp
from jax import lax
from jax.experimental import pallas as pl
from jax.experimental.pallas import tpu as pltpu
from jax.sharding import Mesh, PartitionSpec as P

SWEEPS = 4
NT = 16
HALO = 16
CHUNK = 64
WIDE = CHUNK + 2 * HALO
PIECE = 8
STRIP = 4
NZD = 8
NSP = 16
LANES = 128
BLOCK = 32
F32 = jnp.float32

VMEM = pl.BlockSpec(memory_space=pltpu.VMEM)
LIMIT = 16 * 1024 * 1024
MOST = 60 * 1024 * 1024
BF16 = jnp.bfloat16


def call(kernel, out, specs, scratch=(), mixer=False, sems=(), limit=LIMIT, aliases=None, to=VMEM):
    outs = [jax.ShapeDtypeStruct(s, F32) for s in out]
    scratch = [pltpu.VMEM(s, F32) for s in scratch]
    if mixer:
        scratch.append(pltpu.VMEM((2 * LANES, 2 * LANES), BF16))
    for count in sems:
        scratch.append(pltpu.SemaphoreType.DMA(count))
    return pl.pallas_call(
        kernel,
        out_shape=outs,
        in_specs=specs,
        out_specs=[to] * len(out),
        input_output_aliases=aliases or {},
        scratch_shapes=scratch,
        compiler_params=pltpu.CompilerParams(vmem_limit_bytes=limit),
    )


SNAKE = [x * 4 + (y if x % 2 == 0 else 3 - y) for x in range(4) for y in range(4)]


def position():
    z, core = lax.axis_index("z"), lax.axis_index("core")
    j = lax.axis_index("space")
    x = j // 4
    odd = x % 2
    y = j % 4
    odd_chunk = (y + odd) % 2
    sub = z + odd_chunk * (NZD - 1 - 2 * z)
    return z, core, odd_chunk, sub


def at_ends():
    j = lax.axis_index("space")
    return j == SNAKE[0], j == SNAKE[-1]


def flat(z, core, j):
    return (z * 2 + core) * NSP + j


def piece_pairs(first):
    path = [
        (z, SNAKE[k])
        for k in range(NSP)
        for z in (range(NZD) if k % 2 == 0 else range(NZD - 1, -1, -1))
    ]
    pairs = []
    for core in (0, 1):
        for q in range(first, len(path), 2):
            (z, j), (other_z, other_j) = path[q], path[(q + 1) % len(path)]
            a, b = flat(z, core, j), flat(other_z, core, other_j)
            pairs += [(a, b), (b, a)]
    return pairs


def chunk_pairs(first):
    pairs = []
    for k in range(first, NSP, 2):
        a, b = SNAKE[k], SNAKE[(k + 1) % NSP]
        pairs += [(a, b), (b, a)]
    return pairs


def interval_shift(step):
    moves = []
    for t in range(NT):
        to = (t + step) % NT
        moves += [(flat(t // 2, t % 2, j), flat(to // 2, to % 2, j)) for j in range(NSP)]
    return moves


def edges(rows):
    shape = (1, rows, LANES)
    lane = lax.broadcasted_iota(jnp.int32, shape, 2)
    row = lax.broadcasted_iota(jnp.int32, shape, 1)
    top, bottom = (lane >= 96) & (row < 15), (lane < 32) & (row > 0)
    return (lane & 31) < 31, (lane & 31) > 0, lane >= 96, lane < 32, top, bottom


def rolled(v):
    z_top, z_bottom, x_top, x_bottom, top, bottom = edges(16)
    total = jnp.where(z_top, pltpu.roll(v, LANES - 1, 2), 0.0)
    total = total + jnp.where(z_bottom, pltpu.roll(v, 1, 2), 0.0)
    up = pltpu.roll(v, LANES - 32, 2)
    down = pltpu.roll(v, 32, 2)
    far_up = jnp.where(top, pltpu.roll(up, 15, 1), 0.0)
    far_down = jnp.where(bottom, pltpu.roll(down, 1, 1), 0.0)
    return total + jnp.where(x_top, far_up, up) + jnp.where(x_bottom, far_down, down)


def fill_mixer(m_ref):
    shape = (2 * LANES, 2 * LANES)
    source = lax.broadcasted_iota(jnp.int32, shape, 0) & (LANES - 1)
    column = lax.broadcasted_iota(jnp.int32, shape, 1)
    lane = column & (LANES - 1)
    apart = jnp.abs(source - lane)
    near = ((apart == 1) & ((source >> 5) == (lane >> 5))) | (apart == 32)
    far = apart == 96
    picked = jnp.where(column < LANES, jnp.where(near, 1.0, 0.0), jnp.where(far, 1.0, 0.0))
    m_ref[...] = picked.astype(BF16)


def mixed(v, m_ref):
    n = v.shape[0]
    _, _, _, _, top, bottom = edges(16)
    x = v.reshape(n * 16, LANES)
    high = x.astype(BF16)
    rest = x - high.astype(F32)
    middle = rest.astype(BF16)
    low = (rest - middle.astype(F32)).astype(BF16)
    both = jnp.concatenate([high, middle], 1)
    p = jnp.dot(both, m_ref[...], preferred_element_type=F32)
    p = p + jnp.dot(low, m_ref[:LANES], preferred_element_type=F32)
    near = p[:, :LANES].reshape(v.shape)
    far = p[:, LANES:].reshape(v.shape)
    across = jnp.where(bottom, pltpu.roll(far, 1, 1), 0.0)
    return near + jnp.where(top, pltpu.roll(far, 15, 1), across)


def lateral(v, m_ref):
    if m_ref is None:
        return rolled(v)
    sums = []
    for first in range(0, v.shape[0], BLOCK):
        block = v[first : first + BLOCK]
        cut = block.shape[0] // 4
        if cut > 0:
            sums.append(rolled(block[:cut]))
        sums.append(mixed(block[cut:], m_ref))
    return jnp.concatenate(sums, 0)


def swept(v, bb, cc, m_ref=None):
    return bb + cc * (lateral(v[1:-1], m_ref) + v[2:] + v[:-2])


def prep_kernel(c_ref, s_ref, r_ref, out_ref, v_ref, q_ref, o_ref, sems, out_sems):
    zero = jnp.zeros((HALO, LANES), F32)

    def copies(ref, to, first):
        return [
            pltpu.make_async_copy(
                ref.at[:, pl.ds(m * LANES, LANES)], to.at[:, pl.ds(m * LANES, LANES)], sems.at[first + m]
            )
            for m in range(8)
        ]

    def spread(arriving, ref, base):
        leaving = []

        def send(k):
            rows = pl.ds(base, WIDE)
            leaving.append(
                pltpu.make_async_copy(
                    o_ref.at[SNAKE[k], rows], out_ref.at[SNAKE[k], rows], out_sems.at[base // WIDE, k]
                )
            )
            leaving[-1].start()

        o_ref[SNAKE[0], base : base + HALO] = zero
        o_ref[SNAKE[NSP - 1], base + HALO + CHUNK : base + WIDE] = zero
        for m in range(8):
            arriving[m].wait()
            tile = ref[:, m * LANES : (m + 1) * LANES].T
            for half in range(2):
                k = 2 * m + half
                part = tile[half * 64 : half * 64 + 64]
                o_ref[SNAKE[k], base + HALO : base + HALO + CHUNK] = part
                if k > 0:
                    o_ref[SNAKE[k - 1], base + HALO + CHUNK : base + WIDE] = part[:HALO]
                    send(k - 1)
                if k < NSP - 1:
                    o_ref[SNAKE[k + 1], base : base + HALO] = part[CHUNK - HALO :]
        send(NSP - 1)
        return leaving

    def work(ref):
        states, fields = copies(c_ref, v_ref, 0), copies(ref, q_ref, 8)
        for copy in states + fields:
            copy.start()
        leaving = spread(states, v_ref, 0) + spread(fields, q_ref, WIDE)
        for copy in leaving:
            copy.wait()

    core = lax.axis_index("core")

    @pl.when(core == 0)
    def _():
        work(s_ref)

    @pl.when(core != 0)
    def _():
        work(r_ref)


def unpack(base, g_ref, to_ref):
    def one(y, _):
        to_ref[y] = g_ref[pl.ds(base + y, NSP, stride=2 * WIDE), :]
        return 0

    lax.fori_loop(0, WIDE, one, 0, unroll=8)


def field_kernel(g_ref, q_ref):
    unpack(WIDE, g_ref, q_ref)


def state_kernel(g_ref, a_ref, c_ref):
    unpack(0, g_ref, a_ref)
    c_ref[...] = a_ref[HALO : HALO + CHUNK]


def double_step(number, a_ref, b_ref, bb_ref, inv_ref, cc_ref, sinv_ref, m_ref):
    refs = [a_ref, b_ref]
    for step in (number, number + 1):
        edge = step * SWEEPS
        bb_ref[edge : WIDE - edge] = (
            a_ref[edge : WIDE - edge] * inv_ref[edge : WIDE - edge] + sinv_ref[edge : WIDE - edge]
        )
        for sweep in range(SWEEPS):
            src, dst = refs[sweep % 2], refs[(sweep + 1) % 2]
            low = edge + sweep + 1
            high = WIDE - low
            dst[low:high] = swept(src[low - 1 : high + 1], bb_ref[low:high], cc_ref[low:high], m_ref)


def first_kernel(
    _, own_ref, oth_ref, a_ref, u_ref, inv2_ref, cc2_ref, inv_ref, cc_ref, sinv_ref,
    b_ref, bb_ref, rate_ref, m_ref,
):
    _, core, _, sub = position()
    step = 8
    fill_mixer(m_ref)

    def init(n, _):
        at = pl.ds(pl.multiple_of(n * step, step), step)
        own, oth = own_ref[at], oth_ref[at]
        source = jnp.where(core == 0, own, oth)
        rate = jnp.where(core == 0, oth, own)
        inv = 1.0 / (1.0 + 6.0 * rate)
        rate_ref[at] = rate
        inv_ref[at] = inv
        cc_ref[at] = rate * inv
        sinv_ref[at] = source * inv
        return 0

    lax.fori_loop(0, WIDE // step, init, 0)
    double_step(0, a_ref, b_ref, bb_ref, inv_ref, cc_ref, sinv_ref, m_ref)
    u_ref[...] = a_ref[HALO : HALO + CHUNK]
    rate = 2.0 * rate_ref[pl.ds(HALO - PIECE + PIECE * sub, 3 * PIECE)]
    inv = 1.0 / (1.0 + 6.0 * rate)
    inv2_ref[...] = inv
    cc2_ref[...] = rate * inv


def second_kernel(u_ref, inv_ref, cc_ref, sinv_ref, w_ref, a_ref, b_ref, bb_ref, m_ref):
    fill_mixer(m_ref)
    a_ref[...] = u_ref[...]
    double_step(2, a_ref, b_ref, bb_ref, inv_ref, cc_ref, sinv_ref, m_ref)
    w_ref[...] = a_ref[HALO : HALO + CHUNK]


def difference_kernel(w_ref, next_ref, r_ref, *part_refs):
    z, core, odd, _ = position()
    last = (z == NZD - 1) & (core == 1)
    for n in range(NZD):
        part = jnp.where(odd == 1, NZD - 1 - n, n)
        after = next_ref[pl.ds(PIECE * part, PIECE)]
        r = jnp.where(last, after, w_ref[pl.ds(PIECE * part, PIECE)]) - after
        r_ref[n] = r
        part_refs[n // 2][n % 2] = r


def messages(odd, e, r_next, a_ref, b_ref):
    head, tail = r_next[:STRIP], r_next[STRIP:]
    a_ref[:PIECE] = e
    b_ref[:PIECE] = e
    a_ref[PIECE:] = jnp.where(odd == 0, tail, head)
    b_ref[PIECE:] = jnp.where(odd == 0, head, tail)


def residual_kernel(own_ref, oth_ref, r_ref, a_ref, b_ref):
    _, core, _, sub = position()
    for t in range(1, NT):
        n = (t // 2 - 1) % NZD
        r_ref[t] = jnp.where(core == t % 2, own_ref[n], oth_ref[n])
    messages(sub % 2, r_ref[1], r_ref[2], a_ref, b_ref)


def coarse_step(v, inv, cc):
    bb = v * inv
    for sweep in range(SWEEPS):
        low = sweep + 1
        high = bb.shape[0] - low
        v = swept(v, bb[low:high], cc[low:high])
    return v


def chain_step(t, ra_ref, rb_ref, e_ref, r_ref, inv_ref, cc_ref):
    sub = position()[3]
    odd = sub % 2
    bottom, top = at_ends()
    ra, rb = ra_ref[...], rb_ref[...]
    left = jnp.where(bottom & (sub == 0), 0.0, jnp.where(odd == 0, rb, ra))
    right = jnp.where(top & (sub == NZD - 1), 0.0, jnp.where(odd == 0, ra, rb))
    e = jnp.concatenate([left[:PIECE], e_ref[...], right[:PIECE]], 0)
    r1 = jnp.concatenate([left[PIECE:], r_ref[t + 1], right[PIECE:]], 0)
    inv, cc = inv_ref[...], cc_ref[...]
    e1 = coarse_step(e, inv, cc) + r1
    e2 = coarse_step(e1, inv[STRIP:-STRIP], cc[STRIP:-STRIP]) + r_ref[t + 2]
    return e1[STRIP:-STRIP], e2


def chain_kernel(t, ra_ref, rb_ref, e_ref, r_ref, inv_ref, cc_ref, e1_ref, e2_ref, a_ref, b_ref):
    sub = position()[3]
    e1, e2 = chain_step(t, ra_ref, rb_ref, e_ref, r_ref, inv_ref, cc_ref)
    e1_ref[...] = e1
    e2_ref[...] = e2
    messages(sub % 2, e2, r_ref[t + 3], a_ref, b_ref)


def chain_end_kernel(t, ra_ref, rb_ref, r_ref, inv_ref, cc_ref, *refs):
    core = lax.axis_index("core")
    e_refs, o_ref = refs[:-1], refs[-1]
    e1, e2 = chain_step(t, ra_ref, rb_ref, e_refs[-1], r_ref, inv_ref, cc_ref)
    errors = [jnp.zeros(e1.shape, F32)] + [ref[...] for ref in e_refs] + [e1, e2]
    for n in range(NT // 2):
        o_ref[n] = jnp.where(core == 0, errors[2 * n], errors[2 * n + 1])


def keep(o_ref, which, values_ref, low, high):
    def one(y, _):
        o_ref[pl.ds(which * CHUNK + y, NSP, stride=3 * CHUNK), :] = values_ref[y]
        return 0

    lax.fori_loop(low, high, one, 0, unroll=8)


def inner_kernel(
    e_ref, cp_ref, r0_ref, r1_ref, r2_ref, r3_ref, c_ref, inv_ref, cc_ref, sinv_ref, o_ref, edge_ref,
    a_ref, b_ref, bb_ref, m_ref, sems
):
    z, core, odd, _ = position()
    first = (z == 0) & (core == 0)
    fill_mixer(m_ref)
    for n in range(NZD):
        at = n * PIECE
        a_ref[at : at + PIECE] = cp_ref[at : at + PIECE] + e_ref[jnp.where(odd == 1, NZD - 1 - n, n)]

    @pl.when(first)
    def _():
        copy = pltpu.make_async_copy(c_ref, a_ref, sems.at[0])
        copy.start()
        copy.wait()

    bb_ref[...] = a_ref[...] * inv_ref[HALO : HALO + CHUNK] + sinv_ref[HALO : HALO + CHUNK]
    edge_ref[0] = a_ref[: 2 * STRIP]
    edge_ref[1] = a_ref[CHUNK - 2 * STRIP :]
    keep(o_ref, 0, a_ref, 0, CHUNK)
    refs = [a_ref, b_ref]
    for sweep in range(SWEEPS):
        src, dst = refs[sweep % 2], refs[(sweep + 1) % 2]
        low = sweep + 1
        high = CHUNK - low
        dst[low:high] = swept(
            src[low - 1 : high + 1], bb_ref[low:high], cc_ref[HALO + low : HALO + high], m_ref
        )
    keep(o_ref, 1, a_ref, STRIP, CHUNK - STRIP)
    for n in range(NZD):
        r_ref = (r0_ref, r1_ref, r2_ref, r3_ref)[n // 2]
        part = jnp.where(odd == 1, NZD - 1 - n, n)
        for y in range(PIECE):
            row = 2 * CHUNK + part * PIECE + y
            o_ref[pl.ds(row, NSP, stride=3 * CHUNK), :] = jnp.where(first, 0.0, r_ref[n % 2, y])


def outer_kernel(s_ref, edge_ref, ra_ref, rb_ref, inv_ref, cc_ref, sinv_ref, o_ref):
    odd = position()[2]
    bottom, top = at_ends()
    before = jnp.where(bottom, 0.0, jnp.where(odd == 0, rb_ref[...], ra_ref[...]))
    behind = jnp.where(top, 0.0, jnp.where(odd == 0, ra_ref[...], rb_ref[...]))
    v = jnp.concatenate([before, edge_ref[0], edge_ref[1], behind], 0)

    def both(ref):
        start, end = HALO - STRIP, HALO + CHUNK + STRIP
        return jnp.concatenate([ref[start : start + 3 * STRIP], ref[end - 3 * STRIP : end]], 0)

    bb, cc = v * both(inv_ref) + both(sinv_ref), both(cc_ref)
    size = v.shape[0]
    for sweep in range(SWEEPS):
        low = sweep + 1
        v = swept(v, bb[low : size - low], cc[low : size - low])
    for y in range(STRIP):
        o_ref[pl.ds(CHUNK + y, NSP, stride=3 * CHUNK), :] = v[y]
        row = 2 * CHUNK - STRIP + y
        o_ref[pl.ds(row, NSP, stride=3 * CHUNK), :] = v[v.shape[0] - STRIP + y]


def finish_kernel(a_ref, f_ref, r_ref, v_ref, sems):
    copies = []
    for which, to in enumerate((f_ref.at[0], f_ref.at[1], r_ref)):
        for m in range(8):
            low = a_ref[SNAKE[2 * m], which * CHUNK : (which + 1) * CHUNK]
            high = a_ref[SNAKE[2 * m + 1], which * CHUNK : (which + 1) * CHUNK]
            v_ref[which, :, m * LANES : (m + 1) * LANES] = jnp.concatenate([low, high], 0).T
        copies.append(pltpu.make_async_copy(v_ref.at[which], to, sems.at[which]))
        copies[-1].start()
    for copy in copies:
        copy.wait()


def strips_kernel(e_ref, cp_ref, c_ref, a_ref, b_ref, head_ref, tail_ref, sems):
    z, core, odd, _ = position()
    low, high = odd * (NZD - 1), (1 - odd) * (NZD - 1)
    head_ref[...] = cp_ref[:STRIP] + e_ref[low, :STRIP]
    tail_ref[...] = cp_ref[CHUNK - STRIP :] + e_ref[high, STRIP:]

    @pl.when((z == 0) & (core == 0))
    def _():
        copies = [
            pltpu.make_async_copy(c_ref.at[pl.ds(0, STRIP)], head_ref, sems.at[0]),
            pltpu.make_async_copy(c_ref.at[pl.ds(CHUNK - STRIP, STRIP)], tail_ref, sems.at[1]),
        ]
        for copy in copies:
            copy.start()
        for copy in copies:
            copy.wait()

    head, tail = head_ref[...], tail_ref[...]
    a_ref[...] = jnp.where(odd == 0, tail, head)
    b_ref[...] = jnp.where(odd == 0, head, tail)


def body(c_guess, source, rate):
    everyone = ("z", "core", "space")
    anywhere = pl.BlockSpec(memory_space=pltpu.HBM)
    plane = (16, LANES)
    piece = (PIECE,) + plane
    message = (PIECE + STRIP,) + plane

    def swap(v):
        return lax.ppermute(v, "core", [(0, 1), (1, 0)])

    sent = call(
        prep_kernel, [(NSP, 2 * WIDE, LANES)], [anywhere] * 3, [(LANES, 1024)] * 2 + [(NSP, 2 * WIDE, LANES)], sems=((16,), (2, NSP)), limit=MOST, to=anywhere
    )(c_guess.reshape(LANES, -1), source.reshape(LANES, -1), rate.reshape(LANES, -1))[0]
    got = lax.all_to_all(sent, "space", 0, 0).reshape(-1, LANES)
    wide, whole = (WIDE,) + plane, (CHUNK,) + plane
    own = call(field_kernel, [wide], [VMEM])(got)[0]
    oth = swap(own)
    state, c = call(state_kernel, [wide, whole], [VMEM])(got)

    ahead, u, inv2, cc2, inv, cc, sinv = call(
        first_kernel,
        [wide, whole] + [(3 * PIECE,) + plane] * 2 + [wide] * 3,
        [VMEM] * 3,
        [wide] * 3,
        mixer=True,
        aliases={0: 0},
    )(state, own, oth)
    after = lax.ppermute(u, everyone, interval_shift(-1))
    w = call(second_kernel, [whole], [VMEM] * 4, [wide] * 3, mixer=True)(ahead, inv, cc, sinv)[0]
    r, *r_parts = call(difference_kernel, [(NZD,) + piece] + [(2,) + piece] * 4, [VMEM] * 2)(w, after)

    mine = lax.all_to_all(r, "z", 0, 0)
    other = swap(mine)
    res, ma, mb = call(
        residual_kernel, [(NT,) + piece, message, message], [VMEM] * 2
    )(mine, other)
    pairs_a, pairs_b = piece_pairs(0), piece_pairs(1)
    beside = [(u, 1)] + [(part, 2) for part in r_parts]
    moved = []
    errors = [res[1]]
    for turn in range(7):
        t = 2 * turn + 1
        ra = lax.ppermute(ma, everyone, pairs_a)
        rb = lax.ppermute(mb, everyone, pairs_b)
        if turn < len(beside):
            part, step = beside[turn]
            ra, rb, part = lax.optimization_barrier((ra, rb, part))
            moved.append(lax.ppermute(part, everyone, interval_shift(step)))
        if turn == 6:
            break
        e1, e2, ma, mb = call(
            functools.partial(chain_kernel, t), [piece, piece, message, message], [VMEM] * 6
        )(ra, rb, errors[-1], res, inv2, cc2)
        errors += [e1, e2]
        if turn > 0 and turn <= len(beside):
            ma, moved[turn - 1] = lax.optimization_barrier((ma, moved[turn - 1]))
    cpoint, *r_parts = moved
    errors = call(
        functools.partial(chain_end_kernel, NT - 3),
        [(NZD,) + piece],
        [VMEM] * (5 + len(errors)),
    )(ra, rb, res, inv2, cc2, *errors)[0]

    chunk = lax.all_to_all(errors, "z", 0, 0)
    edge = (STRIP,) + plane
    ma, mb = call(strips_kernel, [edge] * 2, [VMEM] * 2 + [anywhere], [edge] * 2, sems=((2,),))(
        chunk, cpoint, c
    )
    ra = lax.ppermute(ma, "space", chunk_pairs(0))
    rb = lax.ppermute(mb, "space", chunk_pairs(1))
    sent, edges_in = call(
        inner_kernel,
        [(NSP * 3 * CHUNK, LANES), (2, 2 * STRIP) + plane],
        [VMEM] * 6 + [anywhere] + [VMEM] * 3,
        [whole] * 3,
        mixer=True,
        sems=((1,),),
    )(chunk, cpoint, *r_parts, c, inv, cc, sinv)
    sent = call(outer_kernel, [(NSP * 3 * CHUNK, LANES)], [VMEM] * 7, aliases={0: 0})(
        sent, edges_in, ra, rb, inv, cc, sinv
    )[0]
    got = lax.all_to_all(sent.reshape(NSP, 3 * CHUNK, LANES), "space", 0, 0)
    fine, residual = call(
        finish_kernel,
        [(2, LANES, 1024), (LANES, 1024)],
        [VMEM],
        [(3, LANES, 1024)],
        sems=((3,),),
        to=anywhere,
    )(got)
    return fine.reshape(1, 2, 4, 32, 1024), residual.reshape(1, 4, 32, 1024)


def solution(mesh):
    inner = Mesh(mesh.devices.reshape(NZD, 2, NSP), ("z", "core", "space"))
    tm = ("z", "core")
    return jax.shard_map(
        body,
        mesh=inner,
        in_specs=(P(tm, "space", None, None), P("space", None, None), P("space", None, None)),
        out_specs=(P(tm, None, "space", None, None), P(tm, "space", None, None)),
        check_vma=False,
    )
```

```python
import functools

import jax
import jax.numpy as jnp
from jax import lax
from jax.experimental import pallas as pl
from jax.experimental.pallas import tpu as pltpu
from jax.sharding import Mesh, PartitionSpec as P

SWEEPS = 4
NT = 16
HALO = 16
CHUNK = 64
WIDE = CHUNK + 2 * HALO
PIECE = 8
STRIP = 4
NZD = 8
NSP = 16
LANES = 128
BLOCK = 32
F32 = jnp.float32

VMEM = pl.BlockSpec(memory_space=pltpu.VMEM)
LIMIT = 16 * 1024 * 1024
MOST = 60 * 1024 * 1024
BF16 = jnp.bfloat16


def call(kernel, out, specs, scratch=(), mixer=False, sems=(), limit=LIMIT, aliases=None, to=VMEM):
    outs = [jax.ShapeDtypeStruct(s, F32) for s in out]
    scratch = [pltpu.VMEM(s, F32) for s in scratch]
    if mixer:
        scratch.append(pltpu.VMEM((2 * LANES, 2 * LANES), BF16))
    for count in sems:
        scratch.append(pltpu.SemaphoreType.DMA(count))
    return pl.pallas_call(
        kernel,
        out_shape=outs,
        in_specs=specs,
        out_specs=[to] * len(out),
        input_output_aliases=aliases or {},
        scratch_shapes=scratch,
        compiler_params=pltpu.CompilerParams(vmem_limit_bytes=limit),
    )


SNAKE = [x * 4 + (y if x % 2 == 0 else 3 - y) for x in range(4) for y in range(4)]


def position():
    z, core = lax.axis_index("z"), lax.axis_index("core")
    j = lax.axis_index("space")
    x = j // 4
    odd = x % 2
    y = j % 4
    odd_chunk = (y + odd) % 2
    sub = z + odd_chunk * (NZD - 1 - 2 * z)
    return z, core, odd_chunk, sub


def at_ends():
    j = lax.axis_index("space")
    return j == SNAKE[0], j == SNAKE[-1]


def flat(z, core, j):
    return (z * 2 + core) * NSP + j


def piece_pairs(first):
    path = [
        (z, SNAKE[k])
        for k in range(NSP)
        for z in (range(NZD) if k % 2 == 0 else range(NZD - 1, -1, -1))
    ]
    pairs = []
    for core in (0, 1):
        for q in range(first, len(path), 2):
            (z, j), (other_z, other_j) = path[q], path[(q + 1) % len(path)]
            a, b = flat(z, core, j), flat(other_z, core, other_j)
            pairs += [(a, b), (b, a)]
    return pairs


def chunk_pairs(first):
    pairs = []
    for k in range(first, NSP, 2):
        a, b = SNAKE[k], SNAKE[(k + 1) % NSP]
        pairs += [(a, b), (b, a)]
    return pairs


def interval_shift(step):
    moves = []
    for t in range(NT):
        to = (t + step) % NT
        moves += [(flat(t // 2, t % 2, j), flat(to // 2, to % 2, j)) for j in range(NSP)]
    return moves


def edges(rows):
    shape = (1, rows, LANES)
    lane = lax.broadcasted_iota(jnp.int32, shape, 2)
    row = lax.broadcasted_iota(jnp.int32, shape, 1)
    top, bottom = (lane >= 96) & (row < 15), (lane < 32) & (row > 0)
    return (lane & 31) < 31, (lane & 31) > 0, lane >= 96, lane < 32, top, bottom


def rolled(v):
    z_top, z_bottom, x_top, x_bottom, top, bottom = edges(16)
    total = jnp.where(z_top, pltpu.roll(v, LANES - 1, 2), 0.0)
    total = total + jnp.where(z_bottom, pltpu.roll(v, 1, 2), 0.0)
    up = pltpu.roll(v, LANES - 32, 2)
    down = pltpu.roll(v, 32, 2)
    far_up = jnp.where(top, pltpu.roll(up, 15, 1), 0.0)
    far_down = jnp.where(bottom, pltpu.roll(down, 1, 1), 0.0)
    return total + jnp.where(x_top, far_up, up) + jnp.where(x_bottom, far_down, down)


def fill_mixer(m_ref):
    shape = (2 * LANES, 2 * LANES)
    source = lax.broadcasted_iota(jnp.int32, shape, 0) & (LANES - 1)
    column = lax.broadcasted_iota(jnp.int32, shape, 1)
    lane = column & (LANES - 1)
    apart = jnp.abs(source - lane)
    near = ((apart == 1) & ((source >> 5) == (lane >> 5))) | (apart == 32)
    far = apart == 96
    picked = jnp.where(column < LANES, jnp.where(near, 1.0, 0.0), jnp.where(far, 1.0, 0.0))
    m_ref[...] = picked.astype(BF16)


def mixed(v, m_ref):
    n = v.shape[0]
    _, _, _, _, top, bottom = edges(16)
    x = v.reshape(n * 16, LANES)
    high = x.astype(BF16)
    rest = x - high.astype(F32)
    middle = rest.astype(BF16)
    low = (rest - middle.astype(F32)).astype(BF16)
    both = jnp.concatenate([high, middle], 1)
    p = jnp.dot(both, m_ref[...], preferred_element_type=F32)
    p = p + jnp.dot(low, m_ref[:LANES], preferred_element_type=F32)
    near = p[:, :LANES].reshape(v.shape)
    far = p[:, LANES:].reshape(v.shape)
    across = jnp.where(bottom, pltpu.roll(far, 1, 1), 0.0)
    return near + jnp.where(top, pltpu.roll(far, 15, 1), across)


def lateral(v, m_ref):
    if m_ref is None:
        return rolled(v)
    sums = []
    for first in range(0, v.shape[0], BLOCK):
        block = v[first : first + BLOCK]
        cut = block.shape[0] // 4
        if cut > 0:
            sums.append(rolled(block[:cut]))
        sums.append(mixed(block[cut:], m_ref))
    return jnp.concatenate(sums, 0)


def swept(v, bb, cc, m_ref=None):
    return bb + cc * (lateral(v[1:-1], m_ref) + v[2:] + v[:-2])


def prep_kernel(c_ref, s_ref, r_ref, out_ref, v_ref, q_ref, o_ref, sems, out_sems):
    zero = jnp.zeros((HALO, LANES), F32)

    def copies(ref, to, first):
        bands = [pl.ds(m * 16, 16) for m in range(8)]
        return [
            pltpu.make_async_copy(ref.at[band], to.at[band], sems.at[first + m])
            for m, band in enumerate(bands)
        ]

    def spread(arriving, ref, base):
        leaving = []
        for copy in arriving:
            copy.wait()

        def send(k):
            rows = pl.ds(base, WIDE)
            leaving.append(
                pltpu.make_async_copy(
                    o_ref.at[SNAKE[k], rows], out_ref.at[SNAKE[k], rows], out_sems.at[base // WIDE, k]
                )
            )
            leaving[-1].start()

        o_ref[SNAKE[0], base : base + HALO] = zero
        o_ref[SNAKE[NSP - 1], base + HALO + CHUNK : base + WIDE] = zero
        for m in range(8):
            tile = ref[:, m * LANES : (m + 1) * LANES].T
            for half in range(2):
                k = 2 * m + half
                part = tile[half * 64 : half * 64 + 64]
                o_ref[SNAKE[k], base + HALO : base + HALO + CHUNK] = part
                if k > 0:
                    o_ref[SNAKE[k - 1], base + HALO + CHUNK : base + WIDE] = part[:HALO]
                    send(k - 1)
                if k < NSP - 1:
                    o_ref[SNAKE[k + 1], base : base + HALO] = part[CHUNK - HALO :]
        send(NSP - 1)
        return leaving

    def work(ref):
        states, fields = copies(c_ref, v_ref, 0), copies(ref, q_ref, 8)
        for copy in states + fields:
            copy.start()
        leaving = spread(states, v_ref, 0) + spread(fields, q_ref, WIDE)
        for copy in leaving:
            copy.wait()

    core = lax.axis_index("core")

    @pl.when(core == 0)
    def _():
        work(s_ref)

    @pl.when(core != 0)
    def _():
        work(r_ref)


def unpack(base, g_ref, to_ref):
    def one(y, _):
        to_ref[y] = g_ref[pl.ds(base + y, NSP, stride=2 * WIDE), :]
        return 0

    lax.fori_loop(0, WIDE, one, 0, unroll=8)


def field_kernel(g_ref, q_ref):
    unpack(WIDE, g_ref, q_ref)


def state_kernel(g_ref, a_ref, c_ref):
    unpack(0, g_ref, a_ref)
    c_ref[...] = a_ref[HALO : HALO + CHUNK]


def double_step(number, a_ref, b_ref, bb_ref, inv_ref, cc_ref, sinv_ref, m_ref):
    refs = [a_ref, b_ref]
    for step in (number, number + 1):
        edge = step * SWEEPS
        bb_ref[edge : WIDE - edge] = (
            a_ref[edge : WIDE - edge] * inv_ref[edge : WIDE - edge] + sinv_ref[edge : WIDE - edge]
        )
        for sweep in range(SWEEPS):
            src, dst = refs[sweep % 2], refs[(sweep + 1) % 2]
            low = edge + sweep + 1
            high = WIDE - low
            dst[low:high] = swept(src[low - 1 : high + 1], bb_ref[low:high], cc_ref[low:high], m_ref)


def first_kernel(
    _, own_ref, oth_ref, a_ref, u_ref, inv2_ref, cc2_ref, inv_ref, cc_ref, sinv_ref,
    b_ref, bb_ref, rate_ref, m_ref,
):
    _, core, _, sub = position()
    step = 8
    fill_mixer(m_ref)

    def init(n, _):
        at = pl.ds(pl.multiple_of(n * step, step), step)
        own, oth = own_ref[at], oth_ref[at]
        source = jnp.where(core == 0, own, oth)
        rate = jnp.where(core == 0, oth, own)
        inv = 1.0 / (1.0 + 6.0 * rate)
        rate_ref[at] = rate
        inv_ref[at] = inv
        cc_ref[at] = rate * inv
        sinv_ref[at] = source * inv
        return 0

    lax.fori_loop(0, WIDE // step, init, 0)
    double_step(0, a_ref, b_ref, bb_ref, inv_ref, cc_ref, sinv_ref, m_ref)
    u_ref[...] = a_ref[HALO : HALO + CHUNK]
    rate = 2.0 * rate_ref[pl.ds(HALO - PIECE + PIECE * sub, 3 * PIECE)]
    inv = 1.0 / (1.0 + 6.0 * rate)
    inv2_ref[...] = inv
    cc2_ref[...] = rate * inv


def second_kernel(u_ref, inv_ref, cc_ref, sinv_ref, w_ref, a_ref, b_ref, bb_ref, m_ref):
    fill_mixer(m_ref)
    a_ref[...] = u_ref[...]
    double_step(2, a_ref, b_ref, bb_ref, inv_ref, cc_ref, sinv_ref, m_ref)
    w_ref[...] = a_ref[HALO : HALO + CHUNK]


def difference_kernel(w_ref, next_ref, r_ref, *part_refs):
    z, core, odd, _ = position()
    last = (z == NZD - 1) & (core == 1)
    for n in range(NZD):
        part = jnp.where(odd == 1, NZD - 1 - n, n)
        after = next_ref[pl.ds(PIECE * part, PIECE)]
        r = jnp.where(last, after, w_ref[pl.ds(PIECE * part, PIECE)]) - after
        r_ref[n] = r
        part_refs[n // 2][n % 2] = r


def messages(odd, e, r_next, a_ref, b_ref):
    head, tail = r_next[:STRIP], r_next[STRIP:]
    a_ref[:PIECE] = e
    b_ref[:PIECE] = e
    a_ref[PIECE:] = jnp.where(odd == 0, tail, head)
    b_ref[PIECE:] = jnp.where(odd == 0, head, tail)


def residual_kernel(own_ref, oth_ref, r_ref, a_ref, b_ref):
    _, core, _, sub = position()
    for t in range(1, NT):
        n = (t // 2 - 1) % NZD
        r_ref[t] = jnp.where(core == t % 2, own_ref[n], oth_ref[n])
    messages(sub % 2, r_ref[1], r_ref[2], a_ref, b_ref)


def coarse_step(v, inv, cc):
    bb = v * inv
    for sweep in range(SWEEPS):
        low = sweep + 1
        high = bb.shape[0] - low
        v = swept(v, bb[low:high], cc[low:high])
    return v


def chain_step(t, ra_ref, rb_ref, e_ref, r_ref, inv_ref, cc_ref):
    sub = position()[3]
    odd = sub % 2
    bottom, top = at_ends()
    ra, rb = ra_ref[...], rb_ref[...]
    left = jnp.where(bottom & (sub == 0), 0.0, jnp.where(odd == 0, rb, ra))
    right = jnp.where(top & (sub == NZD - 1), 0.0, jnp.where(odd == 0, ra, rb))
    e = jnp.concatenate([left[:PIECE], e_ref[...], right[:PIECE]], 0)
    r1 = jnp.concatenate([left[PIECE:], r_ref[t + 1], right[PIECE:]], 0)
    return coarse_step(e, inv_ref[...], cc_ref[...]) + r1


def next_step(t, e1, r_ref, inv_ref, cc_ref):
    return coarse_step(e1, inv_ref[STRIP:-STRIP], cc_ref[STRIP:-STRIP]) + r_ref[t + 2]


def chain_kernel(t, ra_ref, rb_ref, e_ref, r_ref, inv_ref, cc_ref, e1_ref, e2_ref, a_ref, b_ref):
    sub = position()[3]
    e1 = chain_step(t, ra_ref, rb_ref, e_ref, r_ref, inv_ref, cc_ref)
    e1_ref[...] = e1[STRIP:-STRIP]
    e2 = next_step(t, e1, r_ref, inv_ref, cc_ref)
    e2_ref[...] = e2
    messages(sub % 2, e2, r_ref[t + 3], a_ref, b_ref)


def chain_end_kernel(t, ra_ref, rb_ref, r_ref, inv_ref, cc_ref, *refs):
    core = lax.axis_index("core")
    e_refs, o_ref = refs[:-1], refs[-1]
    errors = [jnp.zeros(e_refs[0].shape, F32)] + [ref[...] for ref in e_refs]
    for n in range(NT // 2 - 1):
        o_ref[n] = jnp.where(core == 0, errors[2 * n], errors[2 * n + 1])
    e1 = chain_step(t, ra_ref, rb_ref, e_refs[-1], r_ref, inv_ref, cc_ref)

    @pl.when(core == 0)
    def _():
        o_ref[NT // 2 - 1] = e1[STRIP:-STRIP]

    @pl.when(core != 0)
    def _():
        o_ref[NT // 2 - 1] = next_step(t, e1, r_ref, inv_ref, cc_ref)


def keep(o_ref, which, values_ref, low, high):
    def one(y, _):
        o_ref[pl.ds(which * CHUNK + y, NSP, stride=3 * CHUNK), :] = values_ref[y]
        return 0

    lax.fori_loop(low, high, one, 0, unroll=8)


def inner_kernel(
    e_ref, cp_ref, r0_ref, r1_ref, r2_ref, r3_ref, c_ref, inv_ref, cc_ref, sinv_ref, o_ref, edge_ref,
    a_ref, b_ref, bb_ref, m_ref, sems
):
    z, core, odd, _ = position()
    first = (z == 0) & (core == 0)
    fill_mixer(m_ref)
    for n in range(NZD):
        at = n * PIECE
        a_ref[at : at + PIECE] = cp_ref[at : at + PIECE] + e_ref[jnp.where(odd == 1, NZD - 1 - n, n)]

    @pl.when(first)
    def _():
        copy = pltpu.make_async_copy(c_ref, a_ref, sems.at[0])
        copy.start()
        copy.wait()

    bb_ref[...] = a_ref[...] * inv_ref[HALO : HALO + CHUNK] + sinv_ref[HALO : HALO + CHUNK]
    edge_ref[0] = a_ref[: 2 * STRIP]
    edge_ref[1] = a_ref[CHUNK - 2 * STRIP :]
    keep(o_ref, 0, a_ref, 0, CHUNK)
    refs = [a_ref, b_ref]
    for sweep in range(SWEEPS):
        src, dst = refs[sweep % 2], refs[(sweep + 1) % 2]
        low = sweep + 1
        high = CHUNK - low
        dst[low:high] = swept(
            src[low - 1 : high + 1], bb_ref[low:high], cc_ref[HALO + low : HALO + high], m_ref
        )
    keep(o_ref, 1, a_ref, STRIP, CHUNK - STRIP)
    for n in range(NZD):
        r_ref = (r0_ref, r1_ref, r2_ref, r3_ref)[n // 2]
        part = jnp.where(odd == 1, NZD - 1 - n, n)
        for y in range(PIECE):
            row = 2 * CHUNK + part * PIECE + y
            o_ref[pl.ds(row, NSP, stride=3 * CHUNK), :] = jnp.where(first, 0.0, r_ref[n % 2, y])


def outer_kernel(s_ref, edge_ref, ra_ref, rb_ref, inv_ref, cc_ref, sinv_ref, o_ref):
    odd = position()[2]
    bottom, top = at_ends()
    before = jnp.where(bottom, 0.0, jnp.where(odd == 0, rb_ref[...], ra_ref[...]))
    behind = jnp.where(top, 0.0, jnp.where(odd == 0, ra_ref[...], rb_ref[...]))
    v = jnp.concatenate([before, edge_ref[0], edge_ref[1], behind], 0)

    def both(ref):
        start, end = HALO - STRIP, HALO + CHUNK + STRIP
        return jnp.concatenate([ref[start : start + 3 * STRIP], ref[end - 3 * STRIP : end]], 0)

    bb, cc = v * both(inv_ref) + both(sinv_ref), both(cc_ref)
    size = v.shape[0]
    for sweep in range(SWEEPS):
        low = sweep + 1
        v = swept(v, bb[low : size - low], cc[low : size - low])
    for y in range(STRIP):
        o_ref[pl.ds(CHUNK + y, NSP, stride=3 * CHUNK), :] = v[y]
        row = 2 * CHUNK - STRIP + y
        o_ref[pl.ds(row, NSP, stride=3 * CHUNK), :] = v[v.shape[0] - STRIP + y]


def finish_kernel(a_ref, f_ref, r_ref, v_ref, sems):
    copies = []
    for which, to in enumerate((f_ref.at[0], f_ref.at[1], r_ref)):
        for m in range(8):
            low = a_ref[SNAKE[2 * m], which * CHUNK : (which + 1) * CHUNK]
            high = a_ref[SNAKE[2 * m + 1], which * CHUNK : (which + 1) * CHUNK]
            v_ref[which, :, m * LANES : (m + 1) * LANES] = jnp.concatenate([low, high], 0).T
        copies.append(pltpu.make_async_copy(v_ref.at[which], to, sems.at[which]))
        copies[-1].start()
    for copy in copies:
        copy.wait()


def strips_kernel(e_ref, cp_ref, c_ref, a_ref, b_ref, head_ref, tail_ref, sems):
    z, core, odd, _ = position()
    low, high = odd * (NZD - 1), (1 - odd) * (NZD - 1)
    head_ref[...] = cp_ref[:STRIP] + e_ref[low, :STRIP]
    tail_ref[...] = cp_ref[CHUNK - STRIP :] + e_ref[high, STRIP:]

    @pl.when((z == 0) & (core == 0))
    def _():
        copies = [
            pltpu.make_async_copy(c_ref.at[pl.ds(0, STRIP)], head_ref, sems.at[0]),
            pltpu.make_async_copy(c_ref.at[pl.ds(CHUNK - STRIP, STRIP)], tail_ref, sems.at[1]),
        ]
        for copy in copies:
            copy.start()
        for copy in copies:
            copy.wait()

    head, tail = head_ref[...], tail_ref[...]
    a_ref[...] = jnp.where(odd == 0, tail, head)
    b_ref[...] = jnp.where(odd == 0, head, tail)


def body(c_guess, source, rate):
    everyone = ("z", "core", "space")
    anywhere = pl.BlockSpec(memory_space=pltpu.HBM)
    plane = (16, LANES)
    piece = (PIECE,) + plane
    message = (PIECE + STRIP,) + plane

    def swap(v):
        return lax.ppermute(v, "core", [(0, 1), (1, 0)])

    sent = call(
        prep_kernel, [(NSP, 2 * WIDE, LANES)], [anywhere] * 3, [(LANES, 1024)] * 2 + [(NSP, 2 * WIDE, LANES)], sems=((16,), (2, NSP)), limit=MOST, to=anywhere
    )(c_guess.reshape(LANES, -1), source.reshape(LANES, -1), rate.reshape(LANES, -1))[0]
    got = lax.all_to_all(sent, "space", 0, 0).reshape(-1, LANES)
    wide, whole = (WIDE,) + plane, (CHUNK,) + plane
    own = call(field_kernel, [wide], [VMEM])(got)[0]
    oth = swap(own)
    state, c = call(state_kernel, [wide, whole], [VMEM])(got)

    ahead, u, inv2, cc2, inv, cc, sinv = call(
        first_kernel,
        [wide, whole] + [(3 * PIECE,) + plane] * 2 + [wide] * 3,
        [VMEM] * 3,
        [wide] * 3,
        mixer=True,
        aliases={0: 0},
    )(state, own, oth)
    after = lax.ppermute(u, everyone, interval_shift(-1))
    w = call(second_kernel, [whole], [VMEM] * 4, [wide] * 3, mixer=True)(ahead, inv, cc, sinv)[0]
    r, *r_parts = call(difference_kernel, [(NZD,) + piece] + [(2,) + piece] * 4, [VMEM] * 2)(w, after)

    mine = lax.all_to_all(r, "z", 0, 0)
    other = swap(mine)
    res, ma, mb = call(
        residual_kernel, [(NT,) + piece, message, message], [VMEM] * 2
    )(mine, other)
    pairs_a, pairs_b = piece_pairs(0), piece_pairs(1)
    beside = [(u, 1)] + [(part, 2) for part in r_parts]
    moved = []
    errors = [res[1]]
    for turn in range(7):
        t = 2 * turn + 1
        ra = lax.ppermute(ma, everyone, pairs_a)
        rb = lax.ppermute(mb, everyone, pairs_b)
        if turn < len(beside):
            part, step = beside[turn]
            ra, rb, part = lax.optimization_barrier((ra, rb, part))
            moved.append(lax.ppermute(part, everyone, interval_shift(step)))
        if turn == 6:
            break
        e1, e2, ma, mb = call(
            functools.partial(chain_kernel, t), [piece, piece, message, message], [VMEM] * 6
        )(ra, rb, errors[-1], res, inv2, cc2)
        errors += [e1, e2]
        if turn > 0 and turn <= len(beside):
            ma, moved[turn - 1] = lax.optimization_barrier((ma, moved[turn - 1]))
    cpoint, *r_parts = moved
    errors = call(
        functools.partial(chain_end_kernel, NT - 3),
        [(NZD,) + piece],
        [VMEM] * (5 + len(errors)),
    )(ra, rb, res, inv2, cc2, *errors)[0]

    chunk = lax.all_to_all(errors, "z", 0, 0)
    edge = (STRIP,) + plane
    ma, mb = call(strips_kernel, [edge] * 2, [VMEM] * 2 + [anywhere], [edge] * 2, sems=((2,),))(
        chunk, cpoint, c
    )
    ra = lax.ppermute(ma, "space", chunk_pairs(0))
    rb = lax.ppermute(mb, "space", chunk_pairs(1))
    sent, edges_in = call(
        inner_kernel,
        [(NSP * 3 * CHUNK, LANES), (2, 2 * STRIP) + plane],
        [VMEM] * 6 + [anywhere] + [VMEM] * 3,
        [whole] * 3,
        mixer=True,
        sems=((1,),),
    )(chunk, cpoint, *r_parts, c, inv, cc, sinv)
    sent = call(outer_kernel, [(NSP * 3 * CHUNK, LANES)], [VMEM] * 7, aliases={0: 0})(
        sent, edges_in, ra, rb, inv, cc, sinv
    )[0]
    got = lax.all_to_all(sent.reshape(NSP, 3 * CHUNK, LANES), "space", 0, 0)
    fine, residual = call(
        finish_kernel,
        [(2, LANES, 1024), (LANES, 1024)],
        [VMEM],
        [(3, LANES, 1024)],
        sems=((3,),),
        to=anywhere,
    )(got)
    return fine.reshape(1, 2, 4, 32, 1024), residual.reshape(1, 4, 32, 1024)


def solution(mesh):
    inner = Mesh(mesh.devices.reshape(NZD, 2, NSP), ("z", "core", "space"))
    tm = ("z", "core")
    return jax.shard_map(
        body,
        mesh=inner,
        in_specs=(P(tm, "space", None, None), P("space", None, None), P("space", None, None)),
        out_specs=(P(tm, None, "space", None, None), P(tm, "space", None, None)),
        check_vma=False,
    )
```

```python
import functools

import jax
import jax.numpy as jnp
from jax import lax
from jax.experimental import pallas as pl
from jax.experimental.pallas import tpu as pltpu
from jax.sharding import Mesh, PartitionSpec as P

SWEEPS = 4
NT = 16
HALO = 16
CHUNK = 64
WIDE = CHUNK + 2 * HALO
PIECE = 8
STRIP = 4
NZD = 8
NSP = 16
LANES = 128
BLOCK = 32
F32 = jnp.float32

VMEM = pl.BlockSpec(memory_space=pltpu.VMEM)
LIMIT = 16 * 1024 * 1024
MOST = 60 * 1024 * 1024
BF16 = jnp.bfloat16


def call(kernel, out, specs, scratch=(), mixer=False, sems=(), limit=LIMIT, aliases=None, to=VMEM):
    outs = [jax.ShapeDtypeStruct(s, F32) for s in out]
    scratch = [pltpu.VMEM(s, F32) for s in scratch]
    if mixer:
        scratch.append(pltpu.VMEM((2 * LANES, 2 * LANES), BF16))
    for count in sems:
        scratch.append(pltpu.SemaphoreType.DMA(count))
    return pl.pallas_call(
        kernel,
        out_shape=outs,
        in_specs=specs,
        out_specs=[to] * len(out),
        input_output_aliases=aliases or {},
        scratch_shapes=scratch,
        compiler_params=pltpu.CompilerParams(vmem_limit_bytes=limit),
    )


SNAKE = [x * 4 + (y if x % 2 == 0 else 3 - y) for x in range(4) for y in range(4)]


def position():
    z, core = lax.axis_index("z"), lax.axis_index("core")
    j = lax.axis_index("space")
    x = j // 4
    odd = x % 2
    y = j % 4
    odd_chunk = (y + odd) % 2
    sub = z + odd_chunk * (NZD - 1 - 2 * z)
    return z, core, odd_chunk, sub


def at_ends():
    j = lax.axis_index("space")
    return j == SNAKE[0], j == SNAKE[-1]


def flat(z, core, j):
    return (z * 2 + core) * NSP + j


def piece_pairs(first):
    path = [
        (z, SNAKE[k])
        for k in range(NSP)
        for z in (range(NZD) if k % 2 == 0 else range(NZD - 1, -1, -1))
    ]
    pairs = []
    for core in (0, 1):
        for q in range(first, len(path), 2):
            (z, j), (other_z, other_j) = path[q], path[(q + 1) % len(path)]
            a, b = flat(z, core, j), flat(other_z, core, other_j)
            pairs += [(a, b), (b, a)]
    return pairs


def chunk_pairs(first):
    pairs = []
    for k in range(first, NSP, 2):
        a, b = SNAKE[k], SNAKE[(k + 1) % NSP]
        pairs += [(a, b), (b, a)]
    return pairs


def interval_shift(step):
    moves = []
    for t in range(NT):
        to = (t + step) % NT
        moves += [(flat(t // 2, t % 2, j), flat(to // 2, to % 2, j)) for j in range(NSP)]
    return moves


def edges(rows):
    shape = (1, rows, LANES)
    lane = lax.broadcasted_iota(jnp.int32, shape, 2)
    row = lax.broadcasted_iota(jnp.int32, shape, 1)
    top, bottom = (lane >= 96) & (row < 15), (lane < 32) & (row > 0)
    return (lane & 31) < 31, (lane & 31) > 0, lane >= 96, lane < 32, top, bottom


def rolled(v):
    z_top, z_bottom, x_top, x_bottom, top, bottom = edges(16)
    total = jnp.where(z_top, pltpu.roll(v, LANES - 1, 2), 0.0)
    total = total + jnp.where(z_bottom, pltpu.roll(v, 1, 2), 0.0)
    up = pltpu.roll(v, LANES - 32, 2)
    down = pltpu.roll(v, 32, 2)
    far_up = jnp.where(top, pltpu.roll(up, 15, 1), 0.0)
    far_down = jnp.where(bottom, pltpu.roll(down, 1, 1), 0.0)
    return total + jnp.where(x_top, far_up, up) + jnp.where(x_bottom, far_down, down)


def fill_mixer(m_ref):
    shape = (2 * LANES, 2 * LANES)
    source = lax.broadcasted_iota(jnp.int32, shape, 0) & (LANES - 1)
    column = lax.broadcasted_iota(jnp.int32, shape, 1)
    lane = column & (LANES - 1)
    apart = jnp.abs(source - lane)
    near = ((apart == 1) & ((source >> 5) == (lane >> 5))) | (apart == 32)
    far = apart == 96
    picked = jnp.where(column < LANES, jnp.where(near, 1.0, 0.0), jnp.where(far, 1.0, 0.0))
    m_ref[...] = picked.astype(BF16)


def mixed(v, m_ref):
    n = v.shape[0]
    _, _, _, _, top, bottom = edges(16)
    x = v.reshape(n * 16, LANES)
    high = x.astype(BF16)
    rest = x - high.astype(F32)
    middle = rest.astype(BF16)
    low = (rest - middle.astype(F32)).astype(BF16)
    both = jnp.concatenate([high, middle], 1)
    p = jnp.dot(both, m_ref[...], preferred_element_type=F32)
    p = p + jnp.dot(low, m_ref[:LANES], preferred_element_type=F32)
    near = p[:, :LANES].reshape(v.shape)
    far = p[:, LANES:].reshape(v.shape)
    across = jnp.where(bottom, pltpu.roll(far, 1, 1), 0.0)
    return near + jnp.where(top, pltpu.roll(far, 15, 1), across)


def lateral(v, m_ref):
    if m_ref is None:
        return rolled(v)
    sums = []
    for first in range(0, v.shape[0], BLOCK):
        block = v[first : first + BLOCK]
        cut = block.shape[0] // 4
        if cut > 0:
            sums.append(rolled(block[:cut]))
        sums.append(mixed(block[cut:], m_ref))
    return jnp.concatenate(sums, 0)


def swept(v, bb, cc, m_ref=None):
    return bb + cc * (lateral(v[1:-1], m_ref) + v[2:] + v[:-2])


def prep_kernel(c_ref, s_ref, r_ref, out_ref, v_ref, q_ref, o_ref, sems, out_sems):
    zero = jnp.zeros((HALO, LANES), F32)

    def copies(ref, to, first):
        bands = [pl.ds(m * 16, 16) for m in range(8)]
        return [
            pltpu.make_async_copy(ref.at[band], to.at[band], sems.at[first + m])
            for m, band in enumerate(bands)
        ]

    def spread(arriving, ref, base):
        leaving = []
        for copy in arriving:
            copy.wait()

        def send(k):
            rows = pl.ds(base, WIDE)
            leaving.append(
                pltpu.make_async_copy(
                    o_ref.at[SNAKE[k], rows], out_ref.at[SNAKE[k], rows], out_sems.at[base // WIDE, k]
                )
            )
            leaving[-1].start()

        o_ref[SNAKE[0], base : base + HALO] = zero
        o_ref[SNAKE[NSP - 1], base + HALO + CHUNK : base + WIDE] = zero
        for m in range(8):
            tile = ref[:, m * LANES : (m + 1) * LANES].T
            for half in range(2):
                k = 2 * m + half
                part = tile[half * 64 : half * 64 + 64]
                o_ref[SNAKE[k], base + HALO : base + HALO + CHUNK] = part
                if k > 0:
                    o_ref[SNAKE[k - 1], base + HALO + CHUNK : base + WIDE] = part[:HALO]
                    send(k - 1)
                if k < NSP - 1:
                    o_ref[SNAKE[k + 1], base : base + HALO] = part[CHUNK - HALO :]
        send(NSP - 1)
        return leaving

    def work(ref):
        states, fields = copies(c_ref, v_ref, 0), copies(ref, q_ref, 8)
        for copy in states + fields:
            copy.start()
        leaving = spread(states, v_ref, 0) + spread(fields, q_ref, WIDE)
        for copy in leaving:
            copy.wait()

    core = lax.axis_index("core")

    @pl.when(core == 0)
    def _():
        work(s_ref)

    @pl.when(core != 0)
    def _():
        work(r_ref)


def unpack(base, g_ref, to_ref):
    def one(y, _):
        to_ref[y] = g_ref[pl.ds(base + y, NSP, stride=2 * WIDE), :]
        return 0

    lax.fori_loop(0, WIDE, one, 0, unroll=8)


def field_kernel(g_ref, q_ref):
    unpack(WIDE, g_ref, q_ref)


def state_kernel(g_ref, a_ref, c_ref):
    unpack(0, g_ref, a_ref)
    c_ref[...] = a_ref[HALO : HALO + CHUNK]


def double_step(number, a_ref, b_ref, bb_ref, inv_ref, cc_ref, sinv_ref, m_ref):
    refs = [a_ref, b_ref]
    for step in (number, number + 1):
        edge = step * SWEEPS
        bb_ref[edge : WIDE - edge] = (
            a_ref[edge : WIDE - edge] * inv_ref[edge : WIDE - edge] + sinv_ref[edge : WIDE - edge]
        )
        for sweep in range(SWEEPS):
            src, dst = refs[sweep % 2], refs[(sweep + 1) % 2]
            low = edge + sweep + 1
            high = WIDE - low
            dst[low:high] = swept(src[low - 1 : high + 1], bb_ref[low:high], cc_ref[low:high], m_ref)


def first_kernel(
    _, own_ref, oth_ref, a_ref, u_ref, low_ref, high_ref, inv2_ref, cc2_ref, inv_ref, cc_ref, sinv_ref,
    b_ref, bb_ref, rate_ref, m_ref,
):
    _, core, _, sub = position()
    step = 8
    fill_mixer(m_ref)

    def init(n, _):
        at = pl.ds(pl.multiple_of(n * step, step), step)
        own, oth = own_ref[at], oth_ref[at]
        source = jnp.where(core == 0, own, oth)
        rate = jnp.where(core == 0, oth, own)
        inv = 1.0 / (1.0 + 6.0 * rate)
        rate_ref[at] = rate
        inv_ref[at] = inv
        cc_ref[at] = rate * inv
        sinv_ref[at] = source * inv
        return 0

    lax.fori_loop(0, WIDE // step, init, 0)
    double_step(0, a_ref, b_ref, bb_ref, inv_ref, cc_ref, sinv_ref, m_ref)
    u_ref[...] = a_ref[HALO : HALO + CHUNK]
    low_ref[...] = a_ref[HALO : HALO + CHUNK // 2]
    high_ref[...] = a_ref[HALO + CHUNK // 2 : HALO + CHUNK]
    rate = 2.0 * rate_ref[pl.ds(HALO - PIECE + PIECE * sub, 3 * PIECE)]
    inv = 1.0 / (1.0 + 6.0 * rate)
    inv2_ref[...] = inv
    cc2_ref[...] = rate * inv


def second_kernel(u_ref, inv_ref, cc_ref, sinv_ref, w_ref, a_ref, b_ref, bb_ref, m_ref):
    fill_mixer(m_ref)
    a_ref[...] = u_ref[...]
    double_step(2, a_ref, b_ref, bb_ref, inv_ref, cc_ref, sinv_ref, m_ref)
    w_ref[...] = a_ref[HALO : HALO + CHUNK]


def difference_kernel(w_ref, next_ref, r_ref, *part_refs):
    z, core, odd, _ = position()
    last = (z == NZD - 1) & (core == 1)
    for n in range(NZD):
        part = jnp.where(odd == 1, NZD - 1 - n, n)
        after = next_ref[pl.ds(PIECE * part, PIECE)]
        r = jnp.where(last, after, w_ref[pl.ds(PIECE * part, PIECE)]) - after
        r_ref[n] = r
        part_refs[n // 2][n % 2] = r


def messages(odd, e, r_next, a_ref, b_ref):
    head, tail = r_next[:STRIP], r_next[STRIP:]
    a_ref[:PIECE] = e
    b_ref[:PIECE] = e
    a_ref[PIECE:] = jnp.where(odd == 0, tail, head)
    b_ref[PIECE:] = jnp.where(odd == 0, head, tail)


def residual_kernel(own_ref, oth_ref, r_ref, a_ref, b_ref):
    _, core, _, sub = position()
    for t in range(1, NT):
        n = (t // 2 - 1) % NZD
        r_ref[t] = jnp.where(core == t % 2, own_ref[n], oth_ref[n])
    messages(sub % 2, r_ref[1], r_ref[2], a_ref, b_ref)


def coarse_step(v, inv, cc):
    bb = v * inv
    for sweep in range(SWEEPS):
        low = sweep + 1
        high = bb.shape[0] - low
        v = swept(v, bb[low:high], cc[low:high])
    return v


def chain_step(t, ra_ref, rb_ref, e_ref, r_ref, inv_ref, cc_ref):
    sub = position()[3]
    odd = sub % 2
    bottom, top = at_ends()
    ra, rb = ra_ref[...], rb_ref[...]
    left = jnp.where(bottom & (sub == 0), 0.0, jnp.where(odd == 0, rb, ra))
    right = jnp.where(top & (sub == NZD - 1), 0.0, jnp.where(odd == 0, ra, rb))
    e = jnp.concatenate([left[:PIECE], e_ref[...], right[:PIECE]], 0)
    r1 = jnp.concatenate([left[PIECE:], r_ref[t + 1], right[PIECE:]], 0)
    return coarse_step(e, inv_ref[...], cc_ref[...]) + r1


def next_step(t, e1, r_ref, inv_ref, cc_ref):
    return coarse_step(e1, inv_ref[STRIP:-STRIP], cc_ref[STRIP:-STRIP]) + r_ref[t + 2]


def chain_kernel(t, ra_ref, rb_ref, e_ref, r_ref, inv_ref, cc_ref, e1_ref, e2_ref, a_ref, b_ref):
    sub = position()[3]
    e1 = chain_step(t, ra_ref, rb_ref, e_ref, r_ref, inv_ref, cc_ref)
    e1_ref[...] = e1[STRIP:-STRIP]
    e2 = next_step(t, e1, r_ref, inv_ref, cc_ref)
    e2_ref[...] = e2
    messages(sub % 2, e2, r_ref[t + 3], a_ref, b_ref)


def chain_end_kernel(t, ra_ref, rb_ref, r_ref, inv_ref, cc_ref, *refs):
    core = lax.axis_index("core")
    e_refs, o_ref = refs[:-1], refs[-1]
    errors = [jnp.zeros(e_refs[0].shape, F32)] + [ref[...] for ref in e_refs]
    for n in range(NT // 2 - 1):
        o_ref[n] = jnp.where(core == 0, errors[2 * n], errors[2 * n + 1])
    e1 = chain_step(t, ra_ref, rb_ref, e_refs[-1], r_ref, inv_ref, cc_ref)

    @pl.when(core == 0)
    def _():
        o_ref[NT // 2 - 1] = e1[STRIP:-STRIP]

    @pl.when(core != 0)
    def _():
        o_ref[NT // 2 - 1] = next_step(t, e1, r_ref, inv_ref, cc_ref)


def keep(o_ref, which, values_ref, low, high):
    def one(y, _):
        o_ref[pl.ds(which * CHUNK + y, NSP, stride=3 * CHUNK), :] = values_ref[y]
        return 0

    lax.fori_loop(low, high, one, 0, unroll=8)


def inner_kernel(
    e_ref, cp_low_ref, cp_high_ref, r0_ref, r1_ref, r2_ref, r3_ref, c_ref, inv_ref, cc_ref, sinv_ref, o_ref, edge_ref,
    a_ref, b_ref, bb_ref, m_ref, sems
):
    z, core, odd, _ = position()
    first = (z == 0) & (core == 0)
    fill_mixer(m_ref)
    for n in range(NZD):
        at = n * PIECE
        cp_ref = cp_low_ref if at < CHUNK // 2 else cp_high_ref
        row = at % (CHUNK // 2)
        a_ref[at : at + PIECE] = cp_ref[row : row + PIECE] + e_ref[jnp.where(odd == 1, NZD - 1 - n, n)]

    @pl.when(first)
    def _():
        copy = pltpu.make_async_copy(c_ref, a_ref, sems.at[0])
        copy.start()
        copy.wait()

    bb_ref[...] = a_ref[...] * inv_ref[HALO : HALO + CHUNK] + sinv_ref[HALO : HALO + CHUNK]
    edge_ref[0] = a_ref[: 2 * STRIP]
    edge_ref[1] = a_ref[CHUNK - 2 * STRIP :]
    keep(o_ref, 0, a_ref, 0, CHUNK)
    refs = [a_ref, b_ref]
    for sweep in range(SWEEPS):
        src, dst = refs[sweep % 2], refs[(sweep + 1) % 2]
        low = sweep + 1
        high = CHUNK - low
        dst[low:high] = swept(
            src[low - 1 : high + 1], bb_ref[low:high], cc_ref[HALO + low : HALO + high], m_ref
        )
    keep(o_ref, 1, a_ref, STRIP, CHUNK - STRIP)
    for n in range(NZD):
        r_ref = (r0_ref, r1_ref, r2_ref, r3_ref)[n // 2]
        part = jnp.where(odd == 1, NZD - 1 - n, n)
        for y in range(PIECE):
            row = 2 * CHUNK + part * PIECE + y
            o_ref[pl.ds(row, NSP, stride=3 * CHUNK), :] = jnp.where(first, 0.0, r_ref[n % 2, y])


def outer_kernel(s_ref, edge_ref, ra_ref, rb_ref, inv_ref, cc_ref, sinv_ref, o_ref):
    odd = position()[2]
    bottom, top = at_ends()
    before = jnp.where(bottom, 0.0, jnp.where(odd == 0, rb_ref[...], ra_ref[...]))
    behind = jnp.where(top, 0.0, jnp.where(odd == 0, ra_ref[...], rb_ref[...]))
    v = jnp.concatenate([before, edge_ref[0], edge_ref[1], behind], 0)

    def both(ref):
        start, end = HALO - STRIP, HALO + CHUNK + STRIP
        return jnp.concatenate([ref[start : start + 3 * STRIP], ref[end - 3 * STRIP : end]], 0)

    bb, cc = v * both(inv_ref) + both(sinv_ref), both(cc_ref)
    size = v.shape[0]
    for sweep in range(SWEEPS):
        low = sweep + 1
        v = swept(v, bb[low : size - low], cc[low : size - low])
    for y in range(STRIP):
        o_ref[pl.ds(CHUNK + y, NSP, stride=3 * CHUNK), :] = v[y]
        row = 2 * CHUNK - STRIP + y
        o_ref[pl.ds(row, NSP, stride=3 * CHUNK), :] = v[v.shape[0] - STRIP + y]


def finish_kernel(a_ref, f_ref, r_ref, v_ref, sems):
    copies = []
    for which, to in enumerate((f_ref.at[0], f_ref.at[1], r_ref)):
        for m in range(8):
            low = a_ref[SNAKE[2 * m], which * CHUNK : (which + 1) * CHUNK]
            high = a_ref[SNAKE[2 * m + 1], which * CHUNK : (which + 1) * CHUNK]
            v_ref[which, :, m * LANES : (m + 1) * LANES] = jnp.concatenate([low, high], 0).T
        copies.append(pltpu.make_async_copy(v_ref.at[which], to, sems.at[which]))
        copies[-1].start()
    for copy in copies:
        copy.wait()


def strips_kernel(e_ref, cp_low_ref, cp_high_ref, c_ref, a_ref, b_ref, head_ref, tail_ref, sems):
    z, core, odd, _ = position()
    low, high = odd * (NZD - 1), (1 - odd) * (NZD - 1)
    head_ref[...] = cp_low_ref[:STRIP] + e_ref[low, :STRIP]
    tail_ref[...] = cp_high_ref[CHUNK // 2 - STRIP :] + e_ref[high, STRIP:]

    @pl.when((z == 0) & (core == 0))
    def _():
        copies = [
            pltpu.make_async_copy(c_ref.at[pl.ds(0, STRIP)], head_ref, sems.at[0]),
            pltpu.make_async_copy(c_ref.at[pl.ds(CHUNK - STRIP, STRIP)], tail_ref, sems.at[1]),
        ]
        for copy in copies:
            copy.start()
        for copy in copies:
            copy.wait()

    head, tail = head_ref[...], tail_ref[...]
    a_ref[...] = jnp.where(odd == 0, tail, head)
    b_ref[...] = jnp.where(odd == 0, head, tail)


def body(c_guess, source, rate):
    everyone = ("z", "core", "space")
    anywhere = pl.BlockSpec(memory_space=pltpu.HBM)
    plane = (16, LANES)
    piece = (PIECE,) + plane
    message = (PIECE + STRIP,) + plane

    def swap(v):
        return lax.ppermute(v, "core", [(0, 1), (1, 0)])

    sent = call(
        prep_kernel, [(NSP, 2 * WIDE, LANES)], [anywhere] * 3, [(LANES, 1024)] * 2 + [(NSP, 2 * WIDE, LANES)], sems=((16,), (2, NSP)), limit=MOST, to=anywhere
    )(c_guess.reshape(LANES, -1), source.reshape(LANES, -1), rate.reshape(LANES, -1))[0]
    got = lax.all_to_all(sent, "space", 0, 0).reshape(-1, LANES)
    wide, whole = (WIDE,) + plane, (CHUNK,) + plane
    own = call(field_kernel, [wide], [VMEM])(got)[0]
    oth = swap(own)
    state, c = call(state_kernel, [wide, whole], [VMEM])(got)

    half = (CHUNK // 2,) + plane
    ahead, u, u_low, u_high, inv2, cc2, inv, cc, sinv = call(
        first_kernel,
        [wide, whole, half, half] + [(3 * PIECE,) + plane] * 2 + [wide] * 3,
        [VMEM] * 3,
        [wide] * 3,
        mixer=True,
        aliases={0: 0},
    )(state, own, oth)
    after = lax.ppermute(u, everyone, interval_shift(-1))
    w = call(second_kernel, [whole], [VMEM] * 4, [wide] * 3, mixer=True)(ahead, inv, cc, sinv)[0]
    r, *r_parts = call(difference_kernel, [(NZD,) + piece] + [(2,) + piece] * 4, [VMEM] * 2)(w, after)

    mine = lax.all_to_all(r, "z", 0, 0)
    other = swap(mine)
    res, ma, mb = call(
        residual_kernel, [(NT,) + piece, message, message], [VMEM] * 2
    )(mine, other)
    pairs_a, pairs_b = piece_pairs(0), piece_pairs(1)
    beside = [(u_low, 1)] + [(part, 2) for part in r_parts] + [(u_high, 1)]
    moved = []
    errors = [res[1]]
    for turn in range(7):
        t = 2 * turn + 1
        ra = lax.ppermute(ma, everyone, pairs_a)
        rb = lax.ppermute(mb, everyone, pairs_b)
        if turn < len(beside):
            part, step = beside[turn]
            ra, rb, part = lax.optimization_barrier((ra, rb, part))
            moved.append(lax.ppermute(part, everyone, interval_shift(step)))
        if turn == 6:
            break
        e1, e2, ma, mb = call(
            functools.partial(chain_kernel, t), [piece, piece, message, message], [VMEM] * 6
        )(ra, rb, errors[-1], res, inv2, cc2)
        errors += [e1, e2]
        if turn > 0 and turn <= len(beside):
            ma, moved[turn - 1] = lax.optimization_barrier((ma, moved[turn - 1]))
    cp_low, *r_parts, cp_high = moved
    errors = call(
        functools.partial(chain_end_kernel, NT - 3),
        [(NZD,) + piece],
        [VMEM] * (5 + len(errors)),
    )(ra, rb, res, inv2, cc2, *errors)[0]

    chunk = lax.all_to_all(errors, "z", 0, 0)
    edge = (STRIP,) + plane
    ma, mb = call(strips_kernel, [edge] * 2, [VMEM] * 3 + [anywhere], [edge] * 2, sems=((2,),))(
        chunk, cp_low, cp_high, c
    )
    ra = lax.ppermute(ma, "space", chunk_pairs(0))
    rb = lax.ppermute(mb, "space", chunk_pairs(1))
    sent, edges_in = call(
        inner_kernel,
        [(NSP * 3 * CHUNK, LANES), (2, 2 * STRIP) + plane],
        [VMEM] * 7 + [anywhere] + [VMEM] * 3,
        [whole] * 3,
        mixer=True,
        sems=((1,),),
    )(chunk, cp_low, cp_high, *r_parts, c, inv, cc, sinv)
    sent = call(outer_kernel, [(NSP * 3 * CHUNK, LANES)], [VMEM] * 7, aliases={0: 0})(
        sent, edges_in, ra, rb, inv, cc, sinv
    )[0]
    got = lax.all_to_all(sent.reshape(NSP, 3 * CHUNK, LANES), "space", 0, 0)
    fine, residual = call(
        finish_kernel,
        [(2, LANES, 1024), (LANES, 1024)],
        [VMEM],
        [(3, LANES, 1024)],
        sems=((3,),),
        to=anywhere,
    )(got)
    return fine.reshape(1, 2, 4, 32, 1024), residual.reshape(1, 4, 32, 1024)


def solution(mesh):
    inner = Mesh(mesh.devices.reshape(NZD, 2, NSP), ("z", "core", "space"))
    tm = ("z", "core")
    return jax.shard_map(
        body,
        mesh=inner,
        in_specs=(P(tm, "space", None, None), P("space", None, None), P("space", None, None)),
        out_specs=(P(tm, None, "space", None, None), P(tm, "space", None, None)),
        check_vma=False,
    )
```

```python
import functools

import jax
import jax.numpy as jnp
from jax import lax
from jax.experimental import pallas as pl
from jax.experimental.pallas import tpu as pltpu
from jax.sharding import Mesh, PartitionSpec as P

SWEEPS = 4
NT = 16
HALO = 16
CHUNK = 64
WIDE = CHUNK + 2 * HALO
PIECE = 8
STRIP = 4
NZD = 8
NSP = 16
LANES = 128
BLOCK = 32
F32 = jnp.float32

VMEM = pl.BlockSpec(memory_space=pltpu.VMEM)
LIMIT = 16 * 1024 * 1024
MOST = 60 * 1024 * 1024
BF16 = jnp.bfloat16


def call(kernel, out, specs, scratch=(), mixer=False, sems=(), limit=LIMIT, aliases=None, to=VMEM):
    outs = [jax.ShapeDtypeStruct(s, F32) for s in out]
    scratch = [pltpu.VMEM(s, F32) for s in scratch]
    if mixer:
        scratch.append(pltpu.VMEM((2 * LANES, 2 * LANES), BF16))
    for count in sems:
        scratch.append(pltpu.SemaphoreType.DMA(count))
    return pl.pallas_call(
        kernel,
        out_shape=outs,
        in_specs=specs,
        out_specs=[to] * len(out),
        input_output_aliases=aliases or {},
        scratch_shapes=scratch,
        compiler_params=pltpu.CompilerParams(vmem_limit_bytes=limit),
    )


SNAKE = [x * 4 + (y if x % 2 == 0 else 3 - y) for x in range(4) for y in range(4)]


def position():
    z, core = lax.axis_index("z"), lax.axis_index("core")
    j = lax.axis_index("space")
    x = j // 4
    odd = x % 2
    y = j % 4
    odd_chunk = (y + odd) % 2
    sub = z + odd_chunk * (NZD - 1 - 2 * z)
    return z, core, odd_chunk, sub


def at_ends():
    j = lax.axis_index("space")
    return j == SNAKE[0], j == SNAKE[-1]


def flat(z, core, j):
    return (z * 2 + core) * NSP + j


def piece_pairs(first):
    path = [
        (z, SNAKE[k])
        for k in range(NSP)
        for z in (range(NZD) if k % 2 == 0 else range(NZD - 1, -1, -1))
    ]
    pairs = []
    for core in (0, 1):
        for q in range(first, len(path), 2):
            (z, j), (other_z, other_j) = path[q], path[(q + 1) % len(path)]
            a, b = flat(z, core, j), flat(other_z, core, other_j)
            pairs += [(a, b), (b, a)]
    return pairs


def chunk_pairs(first):
    pairs = []
    for k in range(first, NSP, 2):
        a, b = SNAKE[k], SNAKE[(k + 1) % NSP]
        pairs += [(a, b), (b, a)]
    return pairs


def interval_shift(step):
    moves = []
    for t in range(NT):
        to = (t + step) % NT
        moves += [(flat(t // 2, t % 2, j), flat(to // 2, to % 2, j)) for j in range(NSP)]
    return moves


def edges(rows):
    shape = (1, rows, LANES)
    lane = lax.broadcasted_iota(jnp.int32, shape, 2)
    row = lax.broadcasted_iota(jnp.int32, shape, 1)
    top, bottom = (lane >= 96) & (row < 15), (lane < 32) & (row > 0)
    return (lane & 31) < 31, (lane & 31) > 0, lane >= 96, lane < 32, top, bottom


def rolled(v):
    z_top, z_bottom, x_top, x_bottom, top, bottom = edges(16)
    total = jnp.where(z_top, pltpu.roll(v, LANES - 1, 2), 0.0)
    total = total + jnp.where(z_bottom, pltpu.roll(v, 1, 2), 0.0)
    up = pltpu.roll(v, LANES - 32, 2)
    down = pltpu.roll(v, 32, 2)
    far_up = jnp.where(top, pltpu.roll(up, 15, 1), 0.0)
    far_down = jnp.where(bottom, pltpu.roll(down, 1, 1), 0.0)
    return total + jnp.where(x_top, far_up, up) + jnp.where(x_bottom, far_down, down)


def fill_mixer(m_ref):
    shape = (2 * LANES, 2 * LANES)
    source = lax.broadcasted_iota(jnp.int32, shape, 0) & (LANES - 1)
    column = lax.broadcasted_iota(jnp.int32, shape, 1)
    lane = column & (LANES - 1)
    apart = jnp.abs(source - lane)
    near = ((apart == 1) & ((source >> 5) == (lane >> 5))) | (apart == 32)
    far = apart == 96
    picked = jnp.where(column < LANES, jnp.where(near, 1.0, 0.0), jnp.where(far, 1.0, 0.0))
    m_ref[...] = picked.astype(BF16)


def mixed(v, m_ref):
    n = v.shape[0]
    _, _, _, _, top, bottom = edges(16)
    x = v.reshape(n * 16, LANES)
    high = x.astype(BF16)
    rest = x - high.astype(F32)
    middle = rest.astype(BF16)
    low = (rest - middle.astype(F32)).astype(BF16)
    both = jnp.concatenate([high, middle], 1)
    p = jnp.dot(both, m_ref[...], preferred_element_type=F32)
    p = p + jnp.dot(low, m_ref[:LANES], preferred_element_type=F32)
    near = p[:, :LANES].reshape(v.shape)
    far = p[:, LANES:].reshape(v.shape)
    across = jnp.where(bottom, pltpu.roll(far, 1, 1), 0.0)
    return near + jnp.where(top, pltpu.roll(far, 15, 1), across)


def lateral(v, m_ref):
    if m_ref is None:
        return rolled(v)
    sums = []
    for first in range(0, v.shape[0], BLOCK):
        block = v[first : first + BLOCK]
        cut = block.shape[0] // 4
        if cut > 0:
            sums.append(rolled(block[:cut]))
        sums.append(mixed(block[cut:], m_ref))
    return jnp.concatenate(sums, 0)


def swept(v, bb, cc, m_ref=None):
    return bb + cc * (lateral(v[1:-1], m_ref) + v[2:] + v[:-2])


def prep_kernel(c_ref, s_ref, r_ref, out_ref, v_ref, q_ref, o_ref, sems, out_sems):
    zero = jnp.zeros((HALO, LANES), F32)

    def copies(ref, to, first):
        bands = [pl.ds(m * 16, 16) for m in range(8)]
        return [
            pltpu.make_async_copy(ref.at[band], to.at[band], sems.at[first + m])
            for m, band in enumerate(bands)
        ]

    def spread(arriving, ref, base):
        leaving = []
        for copy in arriving:
            copy.wait()

        def send(k):
            rows = pl.ds(base, WIDE)
            leaving.append(
                pltpu.make_async_copy(
                    o_ref.at[SNAKE[k], rows], out_ref.at[SNAKE[k], rows], out_sems.at[base // WIDE, k]
                )
            )
            leaving[-1].start()

        o_ref[SNAKE[0], base : base + HALO] = zero
        o_ref[SNAKE[NSP - 1], base + HALO + CHUNK : base + WIDE] = zero
        for m in range(8):
            tile = ref[:, m * LANES : (m + 1) * LANES].T
            for half in range(2):
                k = 2 * m + half
                part = tile[half * 64 : half * 64 + 64]
                o_ref[SNAKE[k], base + HALO : base + HALO + CHUNK] = part
                if k > 0:
                    o_ref[SNAKE[k - 1], base + HALO + CHUNK : base + WIDE] = part[:HALO]
                    send(k - 1)
                if k < NSP - 1:
                    o_ref[SNAKE[k + 1], base : base + HALO] = part[CHUNK - HALO :]
        send(NSP - 1)
        return leaving

    def work(ref):
        states, fields = copies(c_ref, v_ref, 0), copies(ref, q_ref, 8)
        for copy in states + fields:
            copy.start()
        leaving = spread(states, v_ref, 0) + spread(fields, q_ref, WIDE)
        for copy in leaving:
            copy.wait()

    core = lax.axis_index("core")

    @pl.when(core == 0)
    def _():
        work(s_ref)

    @pl.when(core != 0)
    def _():
        work(r_ref)


def unpack(base, g_ref, to_ref):
    def one(y, _):
        to_ref[y] = g_ref[pl.ds(base + y, NSP, stride=2 * WIDE), :]
        return 0

    lax.fori_loop(0, WIDE, one, 0, unroll=8)


def field_kernel(g_ref, q_ref):
    unpack(WIDE, g_ref, q_ref)


def state_kernel(g_ref, a_ref, c_ref):
    unpack(0, g_ref, a_ref)
    c_ref[...] = a_ref[HALO : HALO + CHUNK]


def double_step(number, a_ref, b_ref, bb_ref, inv_ref, cc_ref, sinv_ref, m_ref):
    refs = [a_ref, b_ref]
    for step in (number, number + 1):
        edge = step * SWEEPS
        bb_ref[edge : WIDE - edge] = (
            a_ref[edge : WIDE - edge] * inv_ref[edge : WIDE - edge] + sinv_ref[edge : WIDE - edge]
        )
        for sweep in range(SWEEPS):
            src, dst = refs[sweep % 2], refs[(sweep + 1) % 2]
            low = edge + sweep + 1
            high = WIDE - low
            dst[low:high] = swept(src[low - 1 : high + 1], bb_ref[low:high], cc_ref[low:high], m_ref)


def first_kernel(
    _, own_ref, oth_ref, a_ref, u_ref, low_ref, high_ref, inv2_ref, cc2_ref, inv_ref, cc_ref, sinv_ref,
    b_ref, bb_ref, rate_ref, m_ref,
):
    _, core, _, sub = position()
    step = 8
    fill_mixer(m_ref)

    def init(n, _):
        at = pl.ds(pl.multiple_of(n * step, step), step)
        own, oth = own_ref[at], oth_ref[at]
        source = jnp.where(core == 0, own, oth)
        rate = jnp.where(core == 0, oth, own)
        inv = 1.0 / (1.0 + 6.0 * rate)
        rate_ref[at] = rate
        inv_ref[at] = inv
        cc_ref[at] = rate * inv
        sinv_ref[at] = source * inv
        return 0

    lax.fori_loop(0, WIDE // step, init, 0)
    double_step(0, a_ref, b_ref, bb_ref, inv_ref, cc_ref, sinv_ref, m_ref)
    u_ref[...] = a_ref[HALO : HALO + CHUNK]
    low_ref[...] = a_ref[HALO : HALO + CHUNK // 2]
    high_ref[...] = a_ref[HALO + CHUNK // 2 : HALO + CHUNK]
    rate = 2.0 * rate_ref[pl.ds(HALO - PIECE + PIECE * sub, 3 * PIECE)]
    inv = 1.0 / (1.0 + 6.0 * rate)
    inv2_ref[...] = inv
    cc2_ref[...] = rate * inv


def second_kernel(u_ref, inv_ref, cc_ref, sinv_ref, w_ref, a_ref, b_ref, bb_ref, m_ref):
    fill_mixer(m_ref)
    a_ref[...] = u_ref[...]
    double_step(2, a_ref, b_ref, bb_ref, inv_ref, cc_ref, sinv_ref, m_ref)
    w_ref[...] = a_ref[HALO : HALO + CHUNK]


def difference_kernel(w_ref, next_ref, r_ref, *part_refs):
    z, core, odd, _ = position()
    last = (z == NZD - 1) & (core == 1)
    for n in range(NZD):
        part = jnp.where(odd == 1, NZD - 1 - n, n)
        after = next_ref[pl.ds(PIECE * part, PIECE)]
        r = jnp.where(last, after, w_ref[pl.ds(PIECE * part, PIECE)]) - after
        r_ref[n] = r
        part_refs[n // 2][n % 2] = r


def messages(odd, e, r_next, a_ref, b_ref):
    head, tail = r_next[:STRIP], r_next[STRIP:]
    a_ref[:PIECE] = e
    b_ref[:PIECE] = e
    a_ref[PIECE:] = jnp.where(odd == 0, tail, head)
    b_ref[PIECE:] = jnp.where(odd == 0, head, tail)


def residual_kernel(own_ref, oth_ref, r_ref, a_ref, b_ref):
    _, core, _, sub = position()
    for t in range(1, NT):
        n = (t // 2 - 1) % NZD
        r_ref[t] = jnp.where(core == t % 2, own_ref[n], oth_ref[n])
    messages(sub % 2, r_ref[1], r_ref[2], a_ref, b_ref)


def coarse_step(v, inv, cc):
    bb = v * inv
    for sweep in range(SWEEPS):
        low = sweep + 1
        high = bb.shape[0] - low
        v = swept(v, bb[low:high], cc[low:high])
    return v


def chain_step(t, ra_ref, rb_ref, e_ref, r_ref, inv_ref, cc_ref):
    sub = position()[3]
    odd = sub % 2
    bottom, top = at_ends()
    ra, rb = ra_ref[...], rb_ref[...]
    left = jnp.where(bottom & (sub == 0), 0.0, jnp.where(odd == 0, rb, ra))
    right = jnp.where(top & (sub == NZD - 1), 0.0, jnp.where(odd == 0, ra, rb))
    e = jnp.concatenate([left[:PIECE], e_ref[...], right[:PIECE]], 0)
    r1 = jnp.concatenate([left[PIECE:], r_ref[t + 1], right[PIECE:]], 0)
    return coarse_step(e, inv_ref[...], cc_ref[...]) + r1


def next_step(t, e1, r_ref, inv_ref, cc_ref):
    return coarse_step(e1, inv_ref[STRIP:-STRIP], cc_ref[STRIP:-STRIP]) + r_ref[t + 2]


def chain_kernel(t, ra_ref, rb_ref, e_ref, r_ref, inv_ref, cc_ref, e1_ref, e2_ref, a_ref, b_ref):
    sub = position()[3]
    e1 = chain_step(t, ra_ref, rb_ref, e_ref, r_ref, inv_ref, cc_ref)
    e1_ref[...] = e1[STRIP:-STRIP]
    e2 = next_step(t, e1, r_ref, inv_ref, cc_ref)
    e2_ref[...] = e2
    messages(sub % 2, e2, r_ref[t + 3], a_ref, b_ref)


def chain_end_kernel(t, ra_ref, rb_ref, r_ref, inv_ref, cc_ref, *refs):
    core = lax.axis_index("core")
    e_refs, o_ref = refs[:-1], refs[-1]
    errors = [jnp.zeros(e_refs[0].shape, F32)] + [ref[...] for ref in e_refs]
    for n in range(NT // 2 - 1):
        o_ref[n] = jnp.where(core == 0, errors[2 * n], errors[2 * n + 1])
    e1 = chain_step(t, ra_ref, rb_ref, e_refs[-1], r_ref, inv_ref, cc_ref)

    @pl.when(core == 0)
    def _():
        o_ref[NT // 2 - 1] = e1[STRIP:-STRIP]

    @pl.when(core != 0)
    def _():
        o_ref[NT // 2 - 1] = next_step(t, e1, r_ref, inv_ref, cc_ref)


def keep(o_ref, which, values_ref, low, high):
    def one(y, _):
        o_ref[pl.ds(which * CHUNK + y, NSP, stride=3 * CHUNK), :] = values_ref[y]
        return 0

    lax.fori_loop(low, high, one, 0, unroll=8)


def inner_kernel(
    e_ref, cp_low_ref, cp_high_ref, r0_ref, r1_ref, r2_ref, r3_ref, c_ref, inv_ref, cc_ref, sinv_ref, o_ref, edge_ref,
    a_ref, b_ref, bb_ref, m_ref, sems
):
    z, core, odd, _ = position()
    first = (z == 0) & (core == 0)
    fill_mixer(m_ref)
    for n in range(NZD):
        at = n * PIECE
        cp_ref = cp_low_ref if at < CHUNK // 2 else cp_high_ref
        row = at % (CHUNK // 2)
        a_ref[at : at + PIECE] = cp_ref[row : row + PIECE] + e_ref[jnp.where(odd == 1, NZD - 1 - n, n)]

    @pl.when(first)
    def _():
        copy = pltpu.make_async_copy(c_ref, a_ref, sems.at[0])
        copy.start()
        copy.wait()

    bb_ref[...] = a_ref[...] * inv_ref[HALO : HALO + CHUNK] + sinv_ref[HALO : HALO + CHUNK]
    edge_ref[0] = a_ref[: 2 * STRIP]
    edge_ref[1] = a_ref[CHUNK - 2 * STRIP :]
    keep(o_ref, 0, a_ref, 0, CHUNK)
    refs = [a_ref, b_ref]
    for sweep in range(SWEEPS):
        src, dst = refs[sweep % 2], refs[(sweep + 1) % 2]
        low = sweep + 1
        high = CHUNK - low
        dst[low:high] = swept(
            src[low - 1 : high + 1], bb_ref[low:high], cc_ref[HALO + low : HALO + high], m_ref
        )
    keep(o_ref, 1, a_ref, STRIP, CHUNK - STRIP)
    for n in range(NZD):
        r_ref = (r0_ref, r1_ref, r2_ref, r3_ref)[n // 2]
        part = jnp.where(odd == 1, NZD - 1 - n, n)
        for y in range(PIECE):
            row = 2 * CHUNK + part * PIECE + y
            o_ref[pl.ds(row, NSP, stride=3 * CHUNK), :] = jnp.where(first, 0.0, r_ref[n % 2, y])


def outer_kernel(s_ref, edge_ref, ra_ref, rb_ref, inv_ref, cc_ref, sinv_ref, o_ref):
    odd = position()[2]
    bottom, top = at_ends()
    before = jnp.where(bottom, 0.0, jnp.where(odd == 0, rb_ref[...], ra_ref[...]))
    behind = jnp.where(top, 0.0, jnp.where(odd == 0, ra_ref[...], rb_ref[...]))
    v = jnp.concatenate([before, edge_ref[0], edge_ref[1], behind], 0)

    def both(ref):
        start, end = HALO - STRIP, HALO + CHUNK + STRIP
        return jnp.concatenate([ref[start : start + 3 * STRIP], ref[end - 3 * STRIP : end]], 0)

    bb, cc = v * both(inv_ref) + both(sinv_ref), both(cc_ref)
    size = v.shape[0]
    for sweep in range(SWEEPS):
        low = sweep + 1
        v = swept(v, bb[low : size - low], cc[low : size - low])
    for y in range(STRIP):
        o_ref[pl.ds(CHUNK + y, NSP, stride=3 * CHUNK), :] = v[y]
        row = 2 * CHUNK - STRIP + y
        o_ref[pl.ds(row, NSP, stride=3 * CHUNK), :] = v[v.shape[0] - STRIP + y]


def finish_kernel(a_ref, f_ref, r_ref, v_ref, sems):
    copies = []
    for which, to in enumerate((f_ref.at[0], f_ref.at[1], r_ref)):
        for m in range(8):
            low = a_ref[SNAKE[2 * m], which * CHUNK : (which + 1) * CHUNK]
            high = a_ref[SNAKE[2 * m + 1], which * CHUNK : (which + 1) * CHUNK]
            v_ref[which, :, m * LANES : (m + 1) * LANES] = jnp.concatenate([low, high], 0).T
        copies.append(pltpu.make_async_copy(v_ref.at[which], to, sems.at[which]))
        copies[-1].start()
    for copy in copies:
        copy.wait()


def strips_kernel(e_ref, cp_low_ref, cp_high_ref, c_ref, a_ref, b_ref, head_ref, tail_ref, sems):
    z, core, odd, _ = position()
    low, high = odd * (NZD - 1), (1 - odd) * (NZD - 1)
    head_ref[...] = cp_low_ref[:STRIP] + e_ref[low, :STRIP]
    tail_ref[...] = cp_high_ref[CHUNK // 2 - STRIP :] + e_ref[high, STRIP:]

    @pl.when((z == 0) & (core == 0))
    def _():
        copies = [
            pltpu.make_async_copy(c_ref.at[pl.ds(0, STRIP)], head_ref, sems.at[0]),
            pltpu.make_async_copy(c_ref.at[pl.ds(CHUNK - STRIP, STRIP)], tail_ref, sems.at[1]),
        ]
        for copy in copies:
            copy.start()
        for copy in copies:
            copy.wait()

    head, tail = head_ref[...], tail_ref[...]
    a_ref[...] = jnp.where(odd == 0, tail, head)
    b_ref[...] = jnp.where(odd == 0, head, tail)


def body(c_guess, source, rate):
    everyone = ("z", "core", "space")
    anywhere = pl.BlockSpec(memory_space=pltpu.HBM)
    plane = (16, LANES)
    piece = (PIECE,) + plane
    message = (PIECE + STRIP,) + plane

    def swap(v):
        return lax.ppermute(v, "core", [(0, 1), (1, 0)])

    sent = call(
        prep_kernel, [(NSP, 2 * WIDE, LANES)], [anywhere] * 3, [(LANES, 1024)] * 2 + [(NSP, 2 * WIDE, LANES)], sems=((16,), (2, NSP)), limit=MOST, to=anywhere
    )(c_guess.reshape(LANES, -1), source.reshape(LANES, -1), rate.reshape(LANES, -1))[0]
    got = lax.all_to_all(sent, "space", 0, 0).reshape(-1, LANES)
    wide, whole = (WIDE,) + plane, (CHUNK,) + plane
    own = call(field_kernel, [wide], [VMEM])(got)[0]
    oth = swap(own)
    state, c = call(state_kernel, [wide, whole], [VMEM])(got)

    half = (CHUNK // 2,) + plane
    ahead, u, u_low, u_high, inv2, cc2, inv, cc, sinv = call(
        first_kernel,
        [wide, whole, half, half] + [(3 * PIECE,) + plane] * 2 + [wide] * 3,
        [VMEM] * 3,
        [wide] * 3,
        mixer=True,
        aliases={0: 0},
    )(state, own, oth)
    after = lax.ppermute(u, everyone, interval_shift(-1))
    w = call(second_kernel, [whole], [VMEM] * 4, [wide] * 3, mixer=True)(ahead, inv, cc, sinv)[0]
    r, *r_parts = call(difference_kernel, [(NZD,) + piece] + [(2,) + piece] * 4, [VMEM] * 2)(w, after)

    mine = lax.all_to_all(r, "z", 0, 0)
    other = swap(mine)
    res, ma, mb = call(
        residual_kernel, [(NT,) + piece, message, message], [VMEM] * 2
    )(mine, other)
    pairs_a, pairs_b = piece_pairs(0), piece_pairs(1)
    beside = [(u_low, 1)] + [(part, 2) for part in r_parts] + [(u_high, 1)]
    moved = []
    errors = [res[1]]
    for turn in range(7):
        t = 2 * turn + 1
        ra = lax.ppermute(ma, everyone, pairs_a)
        rb = lax.ppermute(mb, everyone, pairs_b)
        if turn < len(beside):
            part, step = beside[turn]
            ra, rb, part = lax.optimization_barrier((ra, rb, part))
            moved.append(lax.ppermute(part, everyone, interval_shift(step)))
        if turn == 6:
            ra, moved[-1] = lax.optimization_barrier((ra, moved[-1]))
            break
        e1, e2, ma, mb = call(
            functools.partial(chain_kernel, t), [piece, piece, message, message], [VMEM] * 6
        )(ra, rb, errors[-1], res, inv2, cc2)
        errors += [e1, e2]
        if turn > 0 and turn <= len(beside):
            ma, moved[turn - 1] = lax.optimization_barrier((ma, moved[turn - 1]))
    cp_low, *r_parts, cp_high = moved
    errors = call(
        functools.partial(chain_end_kernel, NT - 3),
        [(NZD,) + piece],
        [VMEM] * (5 + len(errors)),
    )(ra, rb, res, inv2, cc2, *errors)[0]

    chunk = lax.all_to_all(errors, "z", 0, 0)
    edge = (STRIP,) + plane
    ma, mb = call(strips_kernel, [edge] * 2, [VMEM] * 3 + [anywhere], [edge] * 2, sems=((2,),))(
        chunk, cp_low, cp_high, c
    )
    ra = lax.ppermute(ma, "space", chunk_pairs(0))
    rb = lax.ppermute(mb, "space", chunk_pairs(1))
    sent, edges_in = call(
        inner_kernel,
        [(NSP * 3 * CHUNK, LANES), (2, 2 * STRIP) + plane],
        [VMEM] * 7 + [anywhere] + [VMEM] * 3,
        [whole] * 3,
        mixer=True,
        sems=((1,),),
    )(chunk, cp_low, cp_high, *r_parts, c, inv, cc, sinv)
    sent = call(outer_kernel, [(NSP * 3 * CHUNK, LANES)], [VMEM] * 7, aliases={0: 0})(
        sent, edges_in, ra, rb, inv, cc, sinv
    )[0]
    got = lax.all_to_all(sent.reshape(NSP, 3 * CHUNK, LANES), "space", 0, 0)
    fine, residual = call(
        finish_kernel,
        [(2, LANES, 1024), (LANES, 1024)],
        [VMEM],
        [(3, LANES, 1024)],
        sems=((3,),),
        to=anywhere,
    )(got)
    return fine.reshape(1, 2, 4, 32, 1024), residual.reshape(1, 4, 32, 1024)


def solution(mesh):
    inner = Mesh(mesh.devices.reshape(NZD, 2, NSP), ("z", "core", "space"))
    tm = ("z", "core")
    return jax.shard_map(
        body,
        mesh=inner,
        in_specs=(P(tm, "space", None, None), P("space", None, None), P("space", None, None)),
        out_specs=(P(tm, None, "space", None, None), P(tm, "space", None, None)),
        check_vma=False,
    )
```
